32 devices in a mesh: row: 4 (over y, x), col: 8 (over z, core).
Axes of the slice: x: 2, y: 2, z: 4, core: 2. Of those that a mesh axis runs over, the one named last changes fastest.
Arguments:
- view_a: bfloat16 [64, 8192], P('col', 'row'), may hold values from -30 to 30
- view_b: bfloat16 [64, 8192], P('row', 'col'), may hold values from -30 to 30
Outputs:
- loss: float32 [], replicated
- grad_a: bfloat16 [64, 8192], P('col', 'row')
- grad_b: bfloat16 [64, 8192], P('row', 'col')
The draws below stay inside these ranges and needn't reach their ends.
All inputs are finite; a program needn't handle non-finite values.
Results may differ from the reference program's by a relative error of at most 0.0062.
Values may be sent and summed in bfloat16 or wider, within the bound.
No kernel may reach another device: no remote copies, remote signals or barrier semaphores. Data moves between devices by JAX's collectives and lax.ppermute only.
A program may use at most 64 MiB of HBM per device.

```python
import jax
import jax.numpy as jnp
from jax import lax

F = 8192
IMAGES = 64
N_ROW = 4


def shared_part(key):
    base = jax.random.fold_in(key, 11)
    return jax.random.normal(base, (IMAGES, F), jnp.float32)


def noise_ramp(key):
    position = lax.iota(jnp.int32, F).astype(jnp.float32) / (F - 1)
    lowest, highest = (0.3, 2.0)
    ramp = jnp.exp(jnp.log(lowest) + (jnp.log(highest) - jnp.log(lowest)) * position)
    jitter = jnp.exp(jax.random.uniform(jax.random.fold_in(key, 13), (F,), jnp.float32, -0.22, 0.22))
    return (ramp * jitter)[None, :]


def one_view(key, salt):
    common = shared_part(key)
    ramp = noise_ramp(key)
    noise = jax.random.normal(jax.random.fold_in(key, salt), (IMAGES, F), jnp.float32)
    scale = jnp.exp(jax.random.uniform(jax.random.fold_in(key, salt + 1), (1, F), jnp.float32, -1.2, 1.2))
    offset = 1.5 * jax.random.normal(jax.random.fold_in(key, salt + 2), (1, F), jnp.float32)
    values = offset + scale * (common + ramp * noise)
    return jnp.clip(values, -30.0, 30.0).astype(jnp.bfloat16)


def draw_view_a(key, part):
    return one_view(key, 21)


def draw_view_b(key, part):
    return one_view(key, 31)


def setup_inputs(seed: int = 0) -> dict:
    key_list = jax.random.split(jax.random.key(seed), 3)
    return {
        "view_a": draw_view_a(jax.random.fold_in(key_list[2], 71), 0),
        "view_b": draw_view_b(jax.random.fold_in(key_list[2], 71), 0),
    }


off_weight = 0.0051
epsilon = 1e-05

def normalize(values):
    values = values.astype(jnp.float32)
    center = lax.optimization_barrier(jnp.mean(values, 0))
    spread = lax.optimization_barrier(jnp.mean(jnp.square(values - center), 0))
    scaled = lax.rsqrt(spread + epsilon)
    return (((values - center) * scaled).astype(jnp.bfloat16), scaled)

def project(term, normed, scaled):
    normal_f = normed.astype(jnp.float32)
    return scaled * (term - lax.optimization_barrier(jnp.mean(term, 0)) - normal_f * lax.optimization_barrier(jnp.mean(term * normal_f, 0)))

def reference(view_a, view_b):
    normed_a, scaled_a = normalize(view_a)
    normed_b, scaled_b = normalize(view_b)
    width = F // N_ROW
    blocks_a = normed_a.reshape(IMAGES, N_ROW, width).transpose(1, 0, 2)
    columns = lax.iota(jnp.int32, F)

    def one_block(carry, inputs):
        loss_sum, term_b = carry
        index, block = inputs
        corr = lax.dot_general(block, normed_b, (((0,), (0,)), ((), ())), preferred_element_type=jnp.float32) / IMAGES
        rows = index * width + lax.iota(jnp.int32, width)
        diag = rows[:, None] == columns[None, :]
        part = jnp.sum(jnp.where(diag, jnp.square(1.0 - corr), off_weight * jnp.square(corr)))
        weights = jnp.where(diag, 2.0 * (corr - 1.0), 2.0 * off_weight * corr).astype(jnp.bfloat16)
        term_a = lax.dot_general(normed_b, weights, (((1,), (1,)), ((), ())), preferred_element_type=jnp.float32)
        term_b = term_b + jnp.dot(block, weights, preferred_element_type=jnp.float32)
        return ((loss_sum + part, term_b), term_a)
    start = (jnp.zeros((), jnp.float32), jnp.zeros((IMAGES, F), jnp.float32))
    indices = lax.iota(jnp.int32, N_ROW)
    (loss_sum, term_b), terms_a = lax.scan(one_block, start, (indices, blocks_a))
    term_a = terms_a.transpose(1, 0, 2).reshape(IMAGES, F)
    grad_a = project(term_a, normed_a, scaled_a).astype(jnp.bfloat16)
    grad_b = project(term_b, normed_b, scaled_b).astype(jnp.bfloat16)
    return (loss_sum / F, grad_a, grad_b)
```

```python
import jax
import jax.numpy as jnp
from jax import lax
from jax.sharding import PartitionSpec as P

off_weight = 0.0051
epsilon = 1e-05

BOTH = ("row", "col")


def normalize(values):
    values = values.astype(jnp.float32)
    center = jnp.mean(values, 0)
    spread = jnp.mean(jnp.square(values - center), 0)
    scaled = lax.rsqrt(spread + epsilon)
    return (((values - center) * scaled).astype(jnp.bfloat16), scaled)


def tiled_body(view_a, view_b):
    whole_a = lax.all_gather(view_a, "col", axis=0, tiled=True)
    whole_b = lax.all_gather(view_b, "row", axis=0, tiled=True)
    normed_a, scaled_a = normalize(whole_a)
    normed_b, scaled_b = normalize(whole_b)
    count = whole_a.shape[0]
    width_a = whole_a.shape[1]
    width_b = whole_b.shape[1]
    corr = (
        lax.dot_general(
            normed_a, normed_b, (((0,), (0,)), ((), ())), preferred_element_type=jnp.float32
        )
        / count
    )
    rows = lax.axis_index("row") * width_a + lax.iota(jnp.int32, width_a)
    columns = lax.axis_index("col") * width_b + lax.iota(jnp.int32, width_b)
    diag = rows[:, None] == columns[None, :]
    partial_loss = jnp.sum(jnp.where(diag, jnp.square(1.0 - corr), off_weight * jnp.square(corr)))
    weights = jnp.where(diag, 2.0 * (corr - 1.0), 2.0 * off_weight * corr).astype(jnp.bfloat16)
    term_a = lax.dot_general(
        normed_b, weights, (((1,), (1,)), ((), ())), preferred_element_type=jnp.float32
    )
    term_b = jnp.dot(normed_a, weights, preferred_element_type=jnp.float32)
    summed_a = lax.psum_scatter(term_a, "col", scatter_dimension=0, tiled=True)
    summed_b = lax.psum_scatter(term_b, "row", scatter_dimension=0, tiled=True)
    share_a = summed_a.shape[0]
    share_b = summed_b.shape[0]
    mine_a = lax.dynamic_slice_in_dim(normed_a, lax.axis_index("col") * share_a, share_a, 0).astype(
        jnp.float32
    )
    mine_b = lax.dynamic_slice_in_dim(normed_b, lax.axis_index("row") * share_b, share_b, 0).astype(
        jnp.float32
    )
    first_a, second_a = lax.psum((jnp.sum(summed_a, 0), jnp.sum(summed_a * mine_a, 0)), "col")
    first_b, second_b = lax.psum((jnp.sum(summed_b, 0), jnp.sum(summed_b * mine_b, 0)), "row")
    grad_a = (scaled_a * (summed_a - first_a / count - mine_a * (second_a / count))).astype(
        jnp.bfloat16
    )
    grad_b = (scaled_b * (summed_b - first_b / count - mine_b * (second_b / count))).astype(
        jnp.bfloat16
    )
    total = lax.psum(partial_loss, ("row", "col"))
    loss = total / (width_a * lax.axis_size("row"))
    return (loss, grad_a, grad_b)


def sibling(value, n_col):
    return lax.ppermute(value, "col", [(c, c ^ 1) for c in range(n_col)])


def flip(value, side, step):
    pairs = []
    for row in range(side):
        for z in range(side):
            pairs.append(((row * side + z) * 2, (row * side + (z ^ step)) * 2))
            pairs.append(((row * side + z) * 2 + 1, ((row ^ step) * side + z) * 2 + 1))
    return lax.ppermute(value, BOTH, pairs)


def across(value, side, step):
    pairs = []
    for row in range(side):
        for z in range(side):
            pairs.append(((row * side + z) * 2, ((row ^ step) * side + z) * 2))
            pairs.append(((row * side + z) * 2 + 1, (row * side + (z ^ step)) * 2 + 1))
    return lax.ppermute(value, BOTH, pairs)


def in_order(pieces, position):
    bit = 1
    while bit < len(pieces):
        on = (position & bit) != 0
        pieces = [jnp.where(on, pieces[i ^ bit], pieces[i]) for i in range(len(pieces))]
        bit *= 2
    return pieces


def rounded(value):
    return lax.reduce_precision(value, exponent_bits=8, mantissa_bits=7)


def split(value):
    high = rounded(value)
    return high.astype(jnp.bfloat16), rounded(value - high).astype(jnp.bfloat16)


def standardize(values):
    values = values.astype(jnp.float32)
    center = jnp.mean(values, 0)
    spread = jnp.mean(jnp.square(values - center), 0)
    scaled = lax.rsqrt(spread + epsilon)
    return (rounded((values - center) * scaled).astype(jnp.bfloat16), scaled)


def meetings(side):
    chips = [(row, z) for row in range(side) for z in range(side)]

    def hops(p, q):
        return bin(p[0] ^ q[0]).count("1") + abs(p[1] - q[1])

    def search(choices, order, used, chosen):
        if len(chosen) == len(order):
            return dict(chosen)
        chip = order[len(chosen)]
        for pair in choices[chip]:
            if all(used[q] < 2 for q in pair):
                for q in pair:
                    used[q] += 1
                found = search(choices, order, used, chosen + [(chip, pair)])
                if found:
                    return found
                for q in pair:
                    used[q] -= 1
        return None

    if side > 6:
        return None
    for limit in range(1, 3 * side):
        choices = {
            p: [
                (q, t)
                for i, q in enumerate(chips)
                for t in chips[i + 1 :]
                if max(hops(p, q), hops(p, t)) <= limit and len({*p, *q, *t}) == side
            ]
            for p in chips
        }
        if all(choices.values()):
            order = sorted(chips, key=lambda p: len(choices[p]))
            found = search(choices, order, dict.fromkeys(chips, 0), [])
            if found:
                return found
    return None


def spread_sums(known, side):
    n_col = 2 * side
    plan = meetings(side)
    if plan is None:
        step = 1
        while step < side:
            known = known + lax.ppermute(known, "col", [(c, c ^ (2 * step)) for c in range(n_col)])
            step *= 2
        return known
    used, pairs = {}, []
    for (row, z), pair in plan.items():
        for core, (from_row, from_z) in enumerate(pair):
            from_core = used.get((from_row, from_z), 0)
            used[from_row, from_z] = from_core + 1
            pairs.append(((from_row * side + from_z) * 2 + from_core, (row * side + z) * 2 + core))
    known = known + lax.ppermute(known, BOTH, pairs)
    return known + sibling(known, n_col)


def gram_body(side, view_a, view_b):
    n_col = 2 * side
    share, width = view_a.shape
    pair, half = view_b.shape
    count = share * n_col
    row = lax.axis_index("row")
    col = lax.axis_index("col")
    z = lax.shift_right_logical(col, 1)
    is_a = (col & 1) == 0
    diagonal = row == z

    give = jnp.where(is_a, jnp.concatenate([view_b[:share], view_b[share:]], 1), view_a)
    got = sibling(give, n_col)
    both_a = jnp.concatenate([view_a, got], 0)
    both_b = jnp.concatenate(
        [jnp.concatenate([got[:, :half], got[:, half:]], 0), view_b], 1
    )
    own = jnp.where(is_a, both_a, both_b)

    pieces = [own] + [flip(own, side, step) for step in range(1, side)]
    mine = jnp.concatenate(in_order(pieces, jnp.where(is_a, z, row)), 0)
    other = sibling(mine, n_col)

    normed, scaled = standardize(mine)
    gram = lax.dot_general(
        normed, normed, (((1,), (1,)), ((), ())), preferred_element_type=jnp.float32
    )
    other_normed, other_scaled = standardize(other)

    normed_f = normed.astype(jnp.float32)
    other_f = other_normed.astype(jnp.float32)
    corr = jnp.mean(normed_f * other_f, 0)
    slope = jnp.where(diagonal, rounded(2.0 * (corr - 1.0)) - 2.0 * off_weight * corr, 0.0)
    extra = (slope * (normed_f - jnp.mean(normed_f, 0) - other_f * corr)).astype(jnp.bfloat16)
    part = jnp.square(1.0 - corr) - off_weight * jnp.square(corr)
    part = jnp.sum(jnp.where(diagonal, part, 0.0).reshape(-1, 128), 0, keepdims=True)

    flat = jnp.concatenate([gram[i * pair : (i + 1) * pair] for i in range(side)], 1)
    block = side * count

    def payload(images, flat, part):
        part = jnp.broadcast_to(part, (pair, 128))
        return jnp.concatenate([images, *split(flat), *split(part)], 1)

    def parts(value):
        value = value.astype(jnp.float32)
        flat = value[:, width : width + block] + value[:, width + block : width + 2 * block]
        part = value[:1, width + 2 * block :]
        return value[:, :width].astype(jnp.bfloat16), flat, part[:, :128] + part[:, 128:]

    def images_of(step):
        return lax.dynamic_slice_in_dim(extra, (row ^ step) * pair, pair, 0)

    landed = [payload(images_of(0), flat, part)]
    landed += [across(payload(images_of(step), flat, part), side, step) for step in range(1, side)]
    sent = payload(*parts(sum(x.astype(jnp.float32) for x in landed)))

    came = sibling(sent, n_col)
    for_a = jnp.where(is_a, came, sent)
    for_b = jnp.where(is_a, sent, came)

    slots = lax.broadcasted_iota(jnp.int32, (2 * side, 128), 0)
    by_z = (slots & (side - 1)) == z
    by_row = (slots & (side - 1)) == row
    counts = slots >= side
    known = jnp.where(by_z, jnp.where(counts, 1.0, parts(for_b)[2]), 0.0)
    known = known + jnp.where(by_row, jnp.where(counts, 1.0, parts(for_a)[2]), 0.0)
    known = spread_sums(known, side)

    all_a = jnp.where(is_a, normed, other_normed)
    all_b = jnp.where(is_a, other_normed[:, :half], normed[:, half:])
    scaled_a = jnp.where(is_a, scaled, other_scaled)
    scaled_b = jnp.where(is_a, other_scaled[:half], scaled[half:])
    extra_a = jnp.where(is_a, for_a[:share, :width], for_a[share:, :width])
    extra_b = jnp.where(is_a, for_b[:, :half], for_b[:, half:width])

    def gradient(sums, normed, scaled, extra, start, images):
        halves = sums[:, width : width + 2 * block]
        halves = jnp.concatenate(
            [halves[:, i * count : (i + 1) * count] for i in range(2 * side)], 0
        )
        term = jnp.dot(halves, normed, preferred_element_type=jnp.float32)
        term = (term[:count] + term[count:]) * (2.0 * off_weight / count)
        normed_f = normed.astype(jnp.float32)
        first = jnp.mean(term, 0)
        second = jnp.mean(term * normed_f, 0)
        term = lax.dynamic_slice_in_dim(term, start, images, 0)
        normed_f = lax.dynamic_slice_in_dim(normed_f, start, images, 0)
        return (scaled * (term - first - normed_f * second + extra.astype(jnp.float32))).astype(
            jnp.bfloat16
        )

    grad_a = gradient(for_a, all_a, scaled_a, extra_a, col * share, share)
    grad_b = gradient(for_b, all_b, scaled_b, extra_b, row * pair, pair)

    on_diagonal = known[:side] / known[side:]
    everywhere = parts(for_a)[1] * parts(for_b)[1] * (off_weight / (count * count))
    everywhere = sum(everywhere[:, i : i + 128] for i in range(0, block, 128))
    loss = jnp.sum(everywhere + jnp.pad(on_diagonal, ((0, pair - side), (0, 0)))) / (width * side)
    return (loss, grad_a, grad_b)


def solution(mesh):
    in_specs = (P("col", "row"), P("row", "col"))
    out_specs = (P(), P("col", "row"), P("row", "col"))
    n_row, n_col = mesh.shape["row"], mesh.shape["col"]
    square = n_col == 2 * n_row and n_row & (n_row - 1) == 0

    def body(view_a, view_b):
        share, width = view_a.shape
        fits = view_b.shape == (2 * share, width // 2) and width % 256 == 0
        fits = fits and share % 8 == 0 and 2 * share >= n_row and n_row * n_col * share % 128 == 0
        if square and fits:
            return gram_body(n_row, view_a, view_b)
        return tiled_body(view_a, view_b)

    return jax.shard_map(body, mesh=mesh, in_specs=in_specs, out_specs=out_specs, check_vma=False)
```

```python
import jax
import jax.numpy as jnp
from jax import lax
from jax.sharding import PartitionSpec as P

off_weight = 0.0051
epsilon = 1e-05

BOTH = ("row", "col")


def normalize(values):
    values = values.astype(jnp.float32)
    center = jnp.mean(values, 0)
    spread = jnp.mean(jnp.square(values - center), 0)
    scaled = lax.rsqrt(spread + epsilon)
    return (((values - center) * scaled).astype(jnp.bfloat16), scaled)


def tiled_body(view_a, view_b):
    whole_a = lax.all_gather(view_a, "col", axis=0, tiled=True)
    whole_b = lax.all_gather(view_b, "row", axis=0, tiled=True)
    normed_a, scaled_a = normalize(whole_a)
    normed_b, scaled_b = normalize(whole_b)
    count = whole_a.shape[0]
    width_a = whole_a.shape[1]
    width_b = whole_b.shape[1]
    corr = (
        lax.dot_general(
            normed_a, normed_b, (((0,), (0,)), ((), ())), preferred_element_type=jnp.float32
        )
        / count
    )
    rows = lax.axis_index("row") * width_a + lax.iota(jnp.int32, width_a)
    columns = lax.axis_index("col") * width_b + lax.iota(jnp.int32, width_b)
    diag = rows[:, None] == columns[None, :]
    partial_loss = jnp.sum(jnp.where(diag, jnp.square(1.0 - corr), off_weight * jnp.square(corr)))
    weights = jnp.where(diag, 2.0 * (corr - 1.0), 2.0 * off_weight * corr).astype(jnp.bfloat16)
    term_a = lax.dot_general(
        normed_b, weights, (((1,), (1,)), ((), ())), preferred_element_type=jnp.float32
    )
    term_b = jnp.dot(normed_a, weights, preferred_element_type=jnp.float32)
    summed_a = lax.psum_scatter(term_a, "col", scatter_dimension=0, tiled=True)
    summed_b = lax.psum_scatter(term_b, "row", scatter_dimension=0, tiled=True)
    share_a = summed_a.shape[0]
    share_b = summed_b.shape[0]
    mine_a = lax.dynamic_slice_in_dim(normed_a, lax.axis_index("col") * share_a, share_a, 0).astype(
        jnp.float32
    )
    mine_b = lax.dynamic_slice_in_dim(normed_b, lax.axis_index("row") * share_b, share_b, 0).astype(
        jnp.float32
    )
    first_a, second_a = lax.psum((jnp.sum(summed_a, 0), jnp.sum(summed_a * mine_a, 0)), "col")
    first_b, second_b = lax.psum((jnp.sum(summed_b, 0), jnp.sum(summed_b * mine_b, 0)), "row")
    grad_a = (scaled_a * (summed_a - first_a / count - mine_a * (second_a / count))).astype(
        jnp.bfloat16
    )
    grad_b = (scaled_b * (summed_b - first_b / count - mine_b * (second_b / count))).astype(
        jnp.bfloat16
    )
    total = lax.psum(partial_loss, ("row", "col"))
    loss = total / (width_a * lax.axis_size("row"))
    return (loss, grad_a, grad_b)


def sibling(value, n_col):
    return lax.ppermute(value, "col", [(c, c ^ 1) for c in range(n_col)])


def flip(value, side, step):
    pairs = []
    for row in range(side):
        for z in range(side):
            pairs.append(((row * side + z) * 2, (row * side + (z ^ step)) * 2))
            pairs.append(((row * side + z) * 2 + 1, ((row ^ step) * side + z) * 2 + 1))
    return lax.ppermute(value, BOTH, pairs)


def across(value, side, step):
    pairs = []
    for row in range(side):
        for z in range(side):
            pairs.append(((row * side + z) * 2, ((row ^ step) * side + z) * 2))
            pairs.append(((row * side + z) * 2 + 1, (row * side + (z ^ step)) * 2 + 1))
    return lax.ppermute(value, BOTH, pairs)


def in_order(pieces, position):
    bit = 1
    while bit < len(pieces):
        on = (position & bit) != 0
        pieces = [jnp.where(on, pieces[i ^ bit], pieces[i]) for i in range(len(pieces))]
        bit *= 2
    return pieces


def rounded(value):
    return lax.reduce_precision(value, exponent_bits=8, mantissa_bits=7)


def split(value):
    high = rounded(value)
    return high.astype(jnp.bfloat16), rounded(value - high).astype(jnp.bfloat16)


def standardize(values):
    values = values.astype(jnp.float32)
    center = jnp.mean(values, 0)
    spread = jnp.mean(jnp.square(values - center), 0)
    scaled = lax.rsqrt(spread + epsilon)
    return (rounded((values - center) * scaled).astype(jnp.bfloat16), scaled)


def meetings(side):
    chips = [(row, z) for row in range(side) for z in range(side)]
    owners = {v: [(r, z, k) for r, z in chips for k in (0, 1) if (r, z)[1 - k] == v] for v in range(side)}
    wanted = {(r, z): [v for v in range(side) if v not in (r, z)] for r, z in chips}

    def hops(p, q):
        return bin(p[0] ^ q[0]).count("1") + abs(p[1] - q[1])

    rounds = []
    while any(wanted.values()):
        asks = []
        for (r, z), left in wanted.items():
            left.sort(key=lambda v: (v - r - 1) % side if r == z else v)
            asks += [((r, z), v) for v in left[-2:]]

        def place(ask, taken, limit, seen):
            for owner in owners[ask[1]]:
                if owner not in seen and hops(owner, ask[0]) <= limit:
                    seen.add(owner)
                    if owner not in taken or place(taken[owner], taken, limit, seen):
                        taken[owner] = ask
                        return True
            return False

        for limit in range(3 * side):
            taken = {}
            if all([place(ask, taken, limit, set()) for ask in asks]):
                break
        heard, pairs = dict.fromkeys(chips, 0), []
        for (r, z, k), (chip, v) in taken.items():
            receiver = (chip[0] * side + chip[1]) * 2 + heard[chip]
            pairs.append(((r * side + z) * 2 + k, receiver))
            heard[chip] += 1
            wanted[chip].remove(v)
        rounds.append(sorted(pairs))
    return rounds


def gram_body(side, view_a, view_b):
    n_col = 2 * side
    share, width = view_a.shape
    pair, half = view_b.shape
    count = share * n_col
    row = lax.axis_index("row")
    col = lax.axis_index("col")
    z = lax.shift_right_logical(col, 1)
    is_a = (col & 1) == 0
    diagonal = row == z

    got_a, got_b = sibling(view_a, n_col), sibling(view_b, n_col)
    own = jnp.where(
        is_a, jnp.concatenate([view_a, got_a], 0), jnp.concatenate([got_b, view_b], 1)
    )

    pieces = [own] + [flip(own, side, step) for step in range(1, side)]
    mine = jnp.concatenate(in_order(pieces, jnp.where(is_a, z, row)), 0)
    other = sibling(mine, n_col)

    normed, scaled = standardize(mine)
    gram = lax.dot_general(
        normed, normed, (((1,), (1,)), ((), ())), preferred_element_type=jnp.float32
    )
    normed, gram, other = lax.optimization_barrier((normed, gram, other))
    other_normed, other_scaled = standardize(other)

    normed_f = normed.astype(jnp.float32)
    other_f = other_normed.astype(jnp.float32)
    corr = jnp.mean(normed_f * other_f, 0)
    slope = jnp.where(diagonal, rounded(2.0 * (corr - 1.0)) - 2.0 * off_weight * corr, 0.0)
    extra = (slope * (normed_f - jnp.mean(normed_f, 0) - other_f * corr)).astype(jnp.bfloat16)
    part = jnp.square(1.0 - corr) - off_weight * jnp.square(corr)
    part = jnp.sum(jnp.where(diagonal, part, 0.0).reshape(-1, 128), 0, keepdims=True)

    lanes = width // side

    def payload(images, gram, part):
        images = [images[:, i * lanes : (i + 1) * lanes] for i in range(side)]
        part = [jnp.broadcast_to(x, (count // 2, 128)) for x in split(part)]
        return jnp.concatenate([jnp.concatenate(images, 0), *split(gram), jnp.concatenate(part, 0)], 1)

    def images_of(step):
        return lax.dynamic_slice_in_dim(extra, (row ^ step) * pair, pair, 0)

    landed = [payload(images_of(0), gram, part)]
    landed += [across(payload(images_of(step), gram, part), side, step) for step in range(1, side)]
    summed = sum(x.astype(jnp.float32) for x in landed)
    gram = summed[:, lanes : lanes + count] + summed[:, lanes + count : lanes + 2 * count]
    part = summed[:1, lanes + 2 * count :] + summed[count // 2 : count // 2 + 1, lanes + 2 * count :]

    sent = jnp.concatenate([summed[:, :lanes].astype(jnp.bfloat16), *split(gram)], 1)
    came = sibling(sent, n_col)
    for_a = jnp.where(is_a, came, sent)
    for_b = jnp.where(is_a, sent, came)

    slots = lax.broadcasted_iota(jnp.int32, (2 * side, 128), 0)
    known = jnp.where((slots & (side - 1)) == jnp.where(is_a, z, row), jnp.where(slots < side, part, 1.0), 0.0)
    known = known + sum(lax.ppermute(known, BOTH, pairs) for pairs in meetings(side))
    known = known + sibling(known, n_col)

    twice = [jnp.where(is_a, normed, other_normed)] * 2
    all_a = jnp.concatenate(twice, 0)
    twice = [jnp.where(is_a, other_normed[:, :half], normed[:, half:])] * 2
    all_b = jnp.concatenate(twice, 0)
    scaled_a = jnp.where(is_a, scaled, other_scaled)
    scaled_b = jnp.where(is_a, other_scaled[:half], scaled[half:])

    def images_in(sums):
        return jnp.concatenate([sums[i * pair : (i + 1) * pair, :lanes] for i in range(side)], 1)

    extra_a = images_in(for_a)
    extra_a = jnp.where(is_a, extra_a[:share], extra_a[share:])
    extra_b = images_in(for_b)
    extra_b = jnp.where(is_a, extra_b[:, :half], extra_b[:, half:])

    def gradient(sums, twice, scaled, extra, start, images):
        halves = sums[:, lanes : lanes + 2 * count]
        term = jnp.dot(halves, twice, preferred_element_type=jnp.float32)
        term = term * (2.0 * off_weight / count)
        normed_f = twice[:count].astype(jnp.float32)
        first = jnp.mean(term, 0)
        second = jnp.mean(term * normed_f, 0)
        term = lax.dynamic_slice_in_dim(term, start, images, 0)
        normed_f = lax.dynamic_slice_in_dim(normed_f, start, images, 0)
        return (scaled * (term - first - normed_f * second + extra.astype(jnp.float32))).astype(
            jnp.bfloat16
        )

    grad_a = gradient(for_a, all_a, scaled_a, extra_a, col * share, share)
    grad_b = gradient(for_b, all_b, scaled_b, extra_b, row * pair, pair)

    def whole(sums):
        sums = sums.astype(jnp.float32)
        return sums[:, lanes : lanes + count] + sums[:, lanes + count : lanes + 2 * count]

    everywhere = whole(for_a) * whole(for_b) * (off_weight / (count * count * width * side))
    on_diagonal = known[:side] * (1.0 / (width * side)) / known[side:]
    everywhere = jnp.sum(jnp.pad(everywhere.reshape(side, pair, count).sum(0), ((0, 0), (0, -count % 128))), 0)
    loss = jnp.sum(everywhere + jnp.sum(on_diagonal, 0))
    return (loss, grad_a, grad_b)


def solution(mesh):
    in_specs = (P("col", "row"), P("row", "col"))
    out_specs = (P(), P("col", "row"), P("row", "col"))
    n_row, n_col = mesh.shape["row"], mesh.shape["col"]
    square = n_col == 2 * n_row and n_row & (n_row - 1) == 0

    def body(view_a, view_b):
        share, width = view_a.shape
        count = share * n_col
        fits = view_b.shape == (2 * share, width // 2) and width % (128 * n_row) == 0
        fits = fits and share % 8 == 0 and count <= 128 and 2 * count % 128 == 0
        if square and fits:
            return gram_body(n_row, view_a, view_b)
        return tiled_body(view_a, view_b)

    return jax.shard_map(body, mesh=mesh, in_specs=in_specs, out_specs=out_specs, check_vma=False)
```

```python
import jax
import jax.numpy as jnp
from jax import lax
from jax.sharding import PartitionSpec as P

off_weight = 0.0051
epsilon = 1e-05

BOTH = ("row", "col")


def normalize(values):
    values = values.astype(jnp.float32)
    center = jnp.mean(values, 0)
    spread = jnp.mean(jnp.square(values - center), 0)
    scaled = lax.rsqrt(spread + epsilon)
    return (((values - center) * scaled).astype(jnp.bfloat16), scaled)


def tiled_body(view_a, view_b):
    whole_a = lax.all_gather(view_a, "col", axis=0, tiled=True)
    whole_b = lax.all_gather(view_b, "row", axis=0, tiled=True)
    normed_a, scaled_a = normalize(whole_a)
    normed_b, scaled_b = normalize(whole_b)
    count = whole_a.shape[0]
    width_a = whole_a.shape[1]
    width_b = whole_b.shape[1]
    corr = (
        lax.dot_general(
            normed_a, normed_b, (((0,), (0,)), ((), ())), preferred_element_type=jnp.float32
        )
        / count
    )
    rows = lax.axis_index("row") * width_a + lax.iota(jnp.int32, width_a)
    columns = lax.axis_index("col") * width_b + lax.iota(jnp.int32, width_b)
    diag = rows[:, None] == columns[None, :]
    partial_loss = jnp.sum(jnp.where(diag, jnp.square(1.0 - corr), off_weight * jnp.square(corr)))
    weights = jnp.where(diag, 2.0 * (corr - 1.0), 2.0 * off_weight * corr).astype(jnp.bfloat16)
    term_a = lax.dot_general(
        normed_b, weights, (((1,), (1,)), ((), ())), preferred_element_type=jnp.float32
    )
    term_b = jnp.dot(normed_a, weights, preferred_element_type=jnp.float32)
    summed_a = lax.psum_scatter(term_a, "col", scatter_dimension=0, tiled=True)
    summed_b = lax.psum_scatter(term_b, "row", scatter_dimension=0, tiled=True)
    share_a = summed_a.shape[0]
    share_b = summed_b.shape[0]
    mine_a = lax.dynamic_slice_in_dim(normed_a, lax.axis_index("col") * share_a, share_a, 0).astype(
        jnp.float32
    )
    mine_b = lax.dynamic_slice_in_dim(normed_b, lax.axis_index("row") * share_b, share_b, 0).astype(
        jnp.float32
    )
    first_a, second_a = lax.psum((jnp.sum(summed_a, 0), jnp.sum(summed_a * mine_a, 0)), "col")
    first_b, second_b = lax.psum((jnp.sum(summed_b, 0), jnp.sum(summed_b * mine_b, 0)), "row")
    grad_a = (scaled_a * (summed_a - first_a / count - mine_a * (second_a / count))).astype(
        jnp.bfloat16
    )
    grad_b = (scaled_b * (summed_b - first_b / count - mine_b * (second_b / count))).astype(
        jnp.bfloat16
    )
    total = lax.psum(partial_loss, ("row", "col"))
    loss = total / (width_a * lax.axis_size("row"))
    return (loss, grad_a, grad_b)


def sibling(value, n_col):
    return lax.ppermute(value, "col", [(c, c ^ 1) for c in range(n_col)])


def flip(value, side, step):
    pairs = []
    for row in range(side):
        for z in range(side):
            pairs.append(((row * side + z) * 2, (row * side + (z ^ step)) * 2))
            pairs.append(((row * side + z) * 2 + 1, ((row ^ step) * side + z) * 2 + 1))
    return lax.ppermute(value, BOTH, pairs)


def across(value, side, step):
    pairs = []
    for row in range(side):
        for z in range(side):
            pairs.append(((row * side + z) * 2, ((row ^ step) * side + z) * 2))
            pairs.append(((row * side + z) * 2 + 1, (row * side + (z ^ step)) * 2 + 1))
    return lax.ppermute(value, BOTH, pairs)


def in_order(pieces, position):
    bit = 1
    while bit < len(pieces):
        on = (position & bit) != 0
        pieces = [jnp.where(on, pieces[i ^ bit], pieces[i]) for i in range(len(pieces))]
        bit *= 2
    return pieces


def rounded(value):
    return lax.reduce_precision(value, exponent_bits=8, mantissa_bits=7)


def split(value):
    high = rounded(value)
    return high.astype(jnp.bfloat16), rounded(value - high).astype(jnp.bfloat16)


def standardize(values):
    values = values.astype(jnp.float32)
    center = jnp.mean(values, 0)
    spread = jnp.mean(jnp.square(values - center), 0)
    scaled = lax.rsqrt(spread + epsilon)
    return (rounded((values - center) * scaled).astype(jnp.bfloat16), scaled)


def meetings(side):
    chips = [(row, z) for row in range(side) for z in range(side)]

    def hops(p, q):
        return bin(p[0] ^ q[0]).count("1") + abs(p[1] - q[1])

    def search(choices, order, used, chosen):
        if len(chosen) == len(order):
            return dict(chosen)
        chip = order[len(chosen)]
        for pair in choices[chip]:
            if all(used[q] < 2 for q in pair):
                for q in pair:
                    used[q] += 1
                found = search(choices, order, used, chosen + [(chip, pair)])
                if found:
                    return found
                for q in pair:
                    used[q] -= 1
        return None

    if side > 6:
        return None
    for limit in range(1, 3 * side):
        choices = {
            p: [
                (q, t)
                for i, q in enumerate(chips)
                for t in chips[i + 1 :]
                if max(hops(p, q), hops(p, t)) <= limit and len({*p, *q, *t}) == side
            ]
            for p in chips
        }
        if all(choices.values()):
            order = sorted(chips, key=lambda p: len(choices[p]))
            found = search(choices, order, dict.fromkeys(chips, 0), [])
            if found:
                return found
    return None


def hear(known, side):
    plan = meetings(side)
    if plan is None:
        step = 1
        while step < side:
            known = known + lax.ppermute(
                known, "col", [(c, c ^ (2 * step)) for c in range(2 * side)]
            )
            step *= 2
        return known
    used, pairs = {}, []
    for (row, z), pair in plan.items():
        for core, chip in enumerate(pair):
            from_core = used.get(chip, 0)
            used[chip] = from_core + 1
            pairs.append(((chip[0] * side + chip[1]) * 2 + from_core, (row * side + z) * 2 + core))
    return known + lax.ppermute(known, BOTH, pairs)


def gram_body(side, view_a, view_b):
    n_col = 2 * side
    share, width = view_a.shape
    pair, half = view_b.shape
    count = share * n_col
    row = lax.axis_index("row")
    col = lax.axis_index("col")
    z = lax.shift_right_logical(col, 1)
    is_a = (col & 1) == 0
    diagonal = row == z

    got_a, got_b = sibling(view_a, n_col), sibling(view_b, n_col)
    own = jnp.where(
        is_a, jnp.concatenate([view_a, got_a], 0), jnp.concatenate([got_b, view_b], 1)
    )

    pieces = [own] + [flip(own, side, step) for step in range(1, side)]
    mine = jnp.concatenate(in_order(pieces, jnp.where(is_a, z, row)), 0)
    other = sibling(mine, n_col)

    normed, scaled = standardize(mine)
    gram = lax.dot_general(
        normed, normed, (((1,), (1,)), ((), ())), preferred_element_type=jnp.float32
    )
    normed, gram, other = lax.optimization_barrier((normed, gram, other))
    other_normed, other_scaled = standardize(other)

    normed_f = normed.astype(jnp.float32)
    other_f = other_normed.astype(jnp.float32)
    corr = jnp.mean(normed_f * other_f, 0)
    slope = jnp.where(diagonal, rounded(2.0 * (corr - 1.0)) - 2.0 * off_weight * corr, 0.0)
    extra = (slope * (normed_f - jnp.mean(normed_f, 0) - other_f * corr)).astype(jnp.bfloat16)
    part = jnp.square(1.0 - corr) - off_weight * jnp.square(corr)
    part = jnp.sum(jnp.where(diagonal, part, 0.0).reshape(-1, 128), 0, keepdims=True)

    lanes = width // side

    def payload(images, gram, part):
        images = [images[:, i * lanes : (i + 1) * lanes] for i in range(side)]
        part = [jnp.broadcast_to(x, (count // 2, 128)) for x in split(part)]
        return jnp.concatenate([jnp.concatenate(images, 0), *split(gram), jnp.concatenate(part, 0)], 1)

    def images_of(step):
        return lax.dynamic_slice_in_dim(extra, (row ^ step) * pair, pair, 0)

    landed = [payload(images_of(0), gram, part)]
    landed += [across(payload(images_of(step), gram, part), side, step) for step in range(1, side)]
    summed = sum(x.astype(jnp.float32) for x in landed)
    gram = summed[:, lanes : lanes + count] + summed[:, lanes + count : lanes + 2 * count]
    part = summed[:1, lanes + 2 * count :] + summed[count // 2 : count // 2 + 1, lanes + 2 * count :]

    part = jnp.concatenate([jnp.broadcast_to(x, (count // 2, 128)) for x in split(part)], 0)
    sent = jnp.concatenate([summed[:, :lanes].astype(jnp.bfloat16), *split(gram), part], 1)
    came = sibling(sent, n_col)
    for_a = jnp.where(is_a, came, sent)
    for_b = jnp.where(is_a, sent, came)

    def part_of(sums):
        sums = sums[:, lanes + 2 * count :].astype(jnp.float32)
        return sums[:1] + sums[count // 2 : count // 2 + 1]

    slots = lax.broadcasted_iota(jnp.int32, (2 * side, 128), 0)
    block, sums_in = slots & (side - 1), slots < side
    known = jnp.where(block == z, jnp.where(sums_in, part_of(for_b), 1.0), 0.0)
    known = known + jnp.where(block == row, jnp.where(sums_in, part_of(for_a), 1.0), 0.0)
    known = hear(known, side)

    twice = [jnp.where(is_a, normed, other_normed)] * 2
    all_a = jnp.concatenate(twice, 0)
    twice = [jnp.where(is_a, other_normed[:, :half], normed[:, half:])] * 2
    all_b = jnp.concatenate(twice, 0)
    scaled_a = jnp.where(is_a, scaled, other_scaled)
    scaled_b = jnp.where(is_a, other_scaled[:half], scaled[half:])

    def images_in(sums):
        return jnp.concatenate([sums[i * pair : (i + 1) * pair, :lanes] for i in range(side)], 1)

    extra_a = images_in(for_a)
    extra_a = jnp.where(is_a, extra_a[:share], extra_a[share:])
    extra_b = images_in(for_b)
    extra_b = jnp.where(is_a, extra_b[:, :half], extra_b[:, half:])

    def gradient(sums, twice, scaled, extra, start, images):
        halves = sums[:, lanes : lanes + 2 * count]
        term = jnp.dot(halves, twice, preferred_element_type=jnp.float32)
        term = term * (2.0 * off_weight / count)
        normed_f = twice[:count].astype(jnp.float32)
        first = jnp.mean(term, 0)
        second = jnp.mean(term * normed_f, 0)
        term = lax.dynamic_slice_in_dim(term, start, images, 0)
        normed_f = lax.dynamic_slice_in_dim(normed_f, start, images, 0)
        return (scaled * (term - first - normed_f * second + extra.astype(jnp.float32))).astype(
            jnp.bfloat16
        )

    grad_a = gradient(for_a, all_a, scaled_a, extra_a, col * share, share)
    grad_b = gradient(for_b, all_b, scaled_b, extra_b, row * pair, pair)

    def whole(sums):
        sums = sums.astype(jnp.float32)
        return sums[:, lanes : lanes + count] + sums[:, lanes + count : lanes + 2 * count]

    everywhere = whole(for_a) * whole(for_b) * (off_weight / (count * count * width * side))
    everywhere = jnp.pad(jnp.sum(everywhere, 0), (0, 128 - count))
    known, grad_a, grad_b, everywhere = lax.optimization_barrier((known, grad_a, grad_b, everywhere))
    known = known + sibling(known, n_col)
    on_diagonal = known[:side] * (1.0 / (width * side)) / known[side:]
    loss = jnp.sum(everywhere + jnp.sum(on_diagonal, 0))
    return (loss, grad_a, grad_b)


def solution(mesh):
    in_specs = (P("col", "row"), P("row", "col"))
    out_specs = (P(), P("col", "row"), P("row", "col"))
    n_row, n_col = mesh.shape["row"], mesh.shape["col"]
    square = n_col == 2 * n_row and n_row & (n_row - 1) == 0

    def body(view_a, view_b):
        share, width = view_a.shape
        count = share * n_col
        fits = view_b.shape == (2 * share, width // 2) and width % (128 * n_row) == 0
        fits = fits and share % 8 == 0 and count <= 128 and 2 * count % 128 == 0
        if square and fits:
            return gram_body(n_row, view_a, view_b)
        return tiled_body(view_a, view_b)

    return jax.shard_map(body, mesh=mesh, in_specs=in_specs, out_specs=out_specs, check_vma=False)
```

```python
import jax
import jax.numpy as jnp
from jax import lax
from jax.sharding import PartitionSpec as P

off_weight = 0.0051
epsilon = 1e-05

BOTH = ("row", "col")


def normalize(values):
    values = values.astype(jnp.float32)
    center = jnp.mean(values, 0)
    spread = jnp.mean(jnp.square(values - center), 0)
    scaled = lax.rsqrt(spread + epsilon)
    return (((values - center) * scaled).astype(jnp.bfloat16), scaled)


def tiled_body(view_a, view_b):
    whole_a = lax.all_gather(view_a, "col", axis=0, tiled=True)
    whole_b = lax.all_gather(view_b, "row", axis=0, tiled=True)
    normed_a, scaled_a = normalize(whole_a)
    normed_b, scaled_b = normalize(whole_b)
    count = whole_a.shape[0]
    width_a = whole_a.shape[1]
    width_b = whole_b.shape[1]
    corr = (
        lax.dot_general(
            normed_a, normed_b, (((0,), (0,)), ((), ())), preferred_element_type=jnp.float32
        )
        / count
    )
    rows = lax.axis_index("row") * width_a + lax.iota(jnp.int32, width_a)
    columns = lax.axis_index("col") * width_b + lax.iota(jnp.int32, width_b)
    diag = rows[:, None] == columns[None, :]
    partial_loss = jnp.sum(jnp.where(diag, jnp.square(1.0 - corr), off_weight * jnp.square(corr)))
    weights = jnp.where(diag, 2.0 * (corr - 1.0), 2.0 * off_weight * corr).astype(jnp.bfloat16)
    term_a = lax.dot_general(
        normed_b, weights, (((1,), (1,)), ((), ())), preferred_element_type=jnp.float32
    )
    term_b = jnp.dot(normed_a, weights, preferred_element_type=jnp.float32)
    summed_a = lax.psum_scatter(term_a, "col", scatter_dimension=0, tiled=True)
    summed_b = lax.psum_scatter(term_b, "row", scatter_dimension=0, tiled=True)
    share_a = summed_a.shape[0]
    share_b = summed_b.shape[0]
    mine_a = lax.dynamic_slice_in_dim(normed_a, lax.axis_index("col") * share_a, share_a, 0).astype(
        jnp.float32
    )
    mine_b = lax.dynamic_slice_in_dim(normed_b, lax.axis_index("row") * share_b, share_b, 0).astype(
        jnp.float32
    )
    first_a, second_a = lax.psum((jnp.sum(summed_a, 0), jnp.sum(summed_a * mine_a, 0)), "col")
    first_b, second_b = lax.psum((jnp.sum(summed_b, 0), jnp.sum(summed_b * mine_b, 0)), "row")
    grad_a = (scaled_a * (summed_a - first_a / count - mine_a * (second_a / count))).astype(
        jnp.bfloat16
    )
    grad_b = (scaled_b * (summed_b - first_b / count - mine_b * (second_b / count))).astype(
        jnp.bfloat16
    )
    total = lax.psum(partial_loss, ("row", "col"))
    loss = total / (width_a * lax.axis_size("row"))
    return (loss, grad_a, grad_b)


def sibling(value, n_col):
    return lax.ppermute(value, "col", [(c, c ^ 1) for c in range(n_col)])


def flip(value, side, step):
    pairs = []
    for row in range(side):
        for z in range(side):
            pairs.append(((row * side + z) * 2, (row * side + (z ^ step)) * 2))
            pairs.append(((row * side + z) * 2 + 1, ((row ^ step) * side + z) * 2 + 1))
    return lax.ppermute(value, BOTH, pairs)


def across(value, side, step):
    pairs = []
    for row in range(side):
        for z in range(side):
            pairs.append(((row * side + z) * 2, ((row ^ step) * side + z) * 2))
            pairs.append(((row * side + z) * 2 + 1, (row * side + (z ^ step)) * 2 + 1))
    return lax.ppermute(value, BOTH, pairs)


def in_order(pieces, position):
    bit = 1
    while bit < len(pieces):
        on = (position & bit) != 0
        pieces = [jnp.where(on, pieces[i ^ bit], pieces[i]) for i in range(len(pieces))]
        bit *= 2
    return pieces


def rounded(value):
    return lax.reduce_precision(value, exponent_bits=8, mantissa_bits=7)


def split(value):
    high = rounded(value)
    return high.astype(jnp.bfloat16), rounded(value - high).astype(jnp.bfloat16)


def standardize(values):
    values = values.astype(jnp.float32)
    center = jnp.mean(values, 0)
    spread = jnp.mean(jnp.square(values - center), 0)
    scaled = lax.rsqrt(spread + epsilon)
    return (rounded((values - center) * scaled).astype(jnp.bfloat16), scaled)


def early(side):
    return [
        (((v * side + v) * 2 + core), (((v ^ (core + 1)) * side + (v ^ (core + 1))) * 2 + core))
        for v in range(side)
        for core in range(2)
    ]


def meetings(side):
    if side != 4:
        return None
    blocks = set(range(side))
    chips = [(row, z) for row in range(side) for z in range(side)]
    knows = {
        (row, z, core): {(z, row)[core]} | ({row ^ (core + 1)} if row == z else set())
        for row, z in chips
        for core in range(2)
    }

    def hops(p, q):
        return bin(p[0] ^ q[0]).count("1") + abs(p[1] - q[1])

    def search(choices, order, used):
        if not order:
            return []
        for tellers in choices[order[0]]:
            if not used & set(tellers):
                found = search(choices, order[1:], used | set(tellers))
                if found is not None:
                    return [(order[0], tellers)] + found
        return None

    for limit in range(1, 3 * side):
        choices = {}
        for chip in chips:
            own = knows[*chip, 0] | knows[*chip, 1]
            near = [d for d in knows if 0 < hops(d, chip) <= limit]
            tellers = [(d,) for d in near] + [(d, e) for i, d in enumerate(near) for e in near[i + 1 :]]
            choices[chip] = [t for t in tellers if own.union(*(knows[d] for d in t)) == blocks]
        if all(choices.values()):
            order = sorted(chips, key=lambda chip: len(choices[chip]))
            found = search(choices, order, set())
            if found:
                return [
                    ((d[0] * side + d[1]) * 2 + d[2], (chip[0] * side + chip[1]) * 2 + core)
                    for chip, tellers in found
                    for core, d in enumerate(tellers)
                ]
    return None


def gram_body(side, view_a, view_b):
    n_col = 2 * side
    share, width = view_a.shape
    pair, half = view_b.shape
    count = share * n_col
    row = lax.axis_index("row")
    col = lax.axis_index("col")
    z = lax.shift_right_logical(col, 1)
    is_a = (col & 1) == 0
    diagonal = row == z

    got_a, got_b = sibling(view_a, n_col), sibling(view_b, n_col)
    own = jnp.where(
        is_a, jnp.concatenate([view_a, got_a], 0), jnp.concatenate([got_b, view_b], 1)
    )

    pieces = [own] + [flip(own, side, step) for step in range(1, side)]
    mine = jnp.concatenate(in_order(pieces, jnp.where(is_a, z, row)), 0)
    other = sibling(mine, n_col)

    normed, scaled = standardize(mine)
    gram = lax.dot_general(
        normed, normed, (((1,), (1,)), ((), ())), preferred_element_type=jnp.float32
    )
    normed, gram, other = lax.optimization_barrier((normed, gram, other))
    other_normed, other_scaled = standardize(other)

    normed_f = normed.astype(jnp.float32)
    other_f = other_normed.astype(jnp.float32)
    corr = jnp.mean(normed_f * other_f, 0)
    slope = jnp.where(diagonal, rounded(2.0 * (corr - 1.0)) - 2.0 * off_weight * corr, 0.0)
    extra = (slope * (normed_f - jnp.mean(normed_f, 0) - other_f * corr)).astype(jnp.bfloat16)
    part = jnp.square(1.0 - corr) - off_weight * jnp.square(corr)
    part = jnp.sum(jnp.where(diagonal, part, 0.0).reshape(-1, 128), 0, keepdims=True)

    lanes = width // side

    def payload(images, gram, part):
        images = [images[:, i * lanes : (i + 1) * lanes] for i in range(side)]
        part = [jnp.broadcast_to(x, (count // 2, 128)) for x in split(part)]
        return jnp.concatenate([jnp.concatenate(images, 0), *split(gram), jnp.concatenate(part, 0)], 1)

    def images_of(step):
        return lax.dynamic_slice_in_dim(extra, (row ^ step) * pair, pair, 0)

    slots = lax.broadcasted_iota(jnp.int32, (2 * side, 128), 0)

    def in_slot(part, block):
        return jnp.where((slots & (side - 1)) == block, jnp.where(slots < side, part, 1.0), 0.0)

    plan = meetings(side)
    landed = [payload(images_of(0), gram, part)]
    landed += [across(payload(images_of(step), gram, part), side, step) for step in range(1, side)]
    told = 0.0
    if plan:
        told = lax.ppermute(jnp.where(diagonal, in_slot(part, row), 0.0), BOTH, early(side))
    summed = sum(x.astype(jnp.float32) for x in landed)
    gram = summed[:, lanes : lanes + count] + summed[:, lanes + count : lanes + 2 * count]
    part = summed[:1, lanes + 2 * count :] + summed[count // 2 : count // 2 + 1, lanes + 2 * count :]

    sent = jnp.concatenate([summed[:, :lanes].astype(jnp.bfloat16), *split(gram)], 1)
    came = sibling(sent, n_col)
    for_a = jnp.where(is_a, came, sent)
    for_b = jnp.where(is_a, sent, came)

    known = in_slot(part, jnp.where(is_a, z, row)) + told
    heard = jnp.zeros_like(known)
    if plan:
        heard = lax.ppermute(known, BOTH, plan)
    else:
        known = jnp.where(is_a, known, 0.0)
        step = 1
        while step < side:
            known = known + lax.ppermute(known, "col", [(c, c ^ (2 * step)) for c in range(n_col)])
            step *= 2

    twice = [jnp.where(is_a, normed, other_normed)] * 2
    all_a = jnp.concatenate(twice, 0)
    twice = [jnp.where(is_a, other_normed[:, :half], normed[:, half:])] * 2
    all_b = jnp.concatenate(twice, 0)
    scaled_a = jnp.where(is_a, scaled, other_scaled)
    scaled_b = jnp.where(is_a, other_scaled[:half], scaled[half:])

    def images_in(sums):
        return jnp.concatenate([sums[i * pair : (i + 1) * pair, :lanes] for i in range(side)], 1)

    extra_a = images_in(for_a)
    extra_a = jnp.where(is_a, extra_a[:share], extra_a[share:])
    extra_b = images_in(for_b)
    extra_b = jnp.where(is_a, extra_b[:, :half], extra_b[:, half:])

    def terms(sums, twice):
        halves = sums[:, lanes : lanes + 2 * count]
        term = jnp.dot(halves, twice, preferred_element_type=jnp.float32)
        term = term * (2.0 * off_weight / count)
        return (term, jnp.mean(term, 0), jnp.mean(term * twice[:count].astype(jnp.float32), 0))

    def gradient(terms, twice, scaled, extra, start, images):
        term, first, second = terms
        term = lax.dynamic_slice_in_dim(term, start, images, 0)
        normed = lax.dynamic_slice_in_dim(twice, start, images, 0).astype(jnp.float32)
        return (scaled * (term - first - normed * second + extra.astype(jnp.float32))).astype(
            jnp.bfloat16
        )

    def whole(sums):
        sums = sums.astype(jnp.float32)
        return sums[:, lanes : lanes + count] + sums[:, lanes + count : lanes + 2 * count]

    everywhere = whole(for_a) * whole(for_b) * (off_weight / (count * count * width * side))
    everywhere = jnp.pad(jnp.sum(everywhere, 0), (0, 128 - count))
    terms_a, terms_b = terms(for_a, all_a), terms(for_b, all_b)
    heard, terms_a, terms_b, everywhere = lax.optimization_barrier(
        (heard, terms_a, terms_b, everywhere)
    )
    known = known + heard
    known = known + sibling(known, n_col)
    grad_a = gradient(terms_a, all_a, scaled_a, extra_a, col * share, share)
    grad_b = gradient(terms_b, all_b, scaled_b, extra_b, row * pair, pair)
    on_diagonal = known[:side] * (1.0 / (width * side)) / known[side:]
    loss = jnp.sum(everywhere + jnp.sum(on_diagonal, 0))
    return (loss, grad_a, grad_b)


def solution(mesh):
    in_specs = (P("col", "row"), P("row", "col"))
    out_specs = (P(), P("col", "row"), P("row", "col"))
    n_row, n_col = mesh.shape["row"], mesh.shape["col"]
    square = n_col == 2 * n_row and n_row & (n_row - 1) == 0

    def body(view_a, view_b):
        share, width = view_a.shape
        count = share * n_col
        fits = view_b.shape == (2 * share, width // 2) and width % (128 * n_row) == 0
        fits = fits and share % 8 == 0 and count <= 128 and 2 * count % 128 == 0
        if square and fits:
            return gram_body(n_row, view_a, view_b)
        return tiled_body(view_a, view_b)

    return jax.shard_map(body, mesh=mesh, in_specs=in_specs, out_specs=out_specs, check_vma=False)
```

```python
import jax
import jax.numpy as jnp
from jax import lax
from jax.sharding import PartitionSpec as P

off_weight = 0.0051
epsilon = 1e-05

BOTH = ("row", "col")


def normalize(values):
    values = values.astype(jnp.float32)
    center = jnp.mean(values, 0)
    spread = jnp.mean(jnp.square(values - center), 0)
    scaled = lax.rsqrt(spread + epsilon)
    return (((values - center) * scaled).astype(jnp.bfloat16), scaled)


def tiled_body(view_a, view_b):
    whole_a = lax.all_gather(view_a, "col", axis=0, tiled=True)
    whole_b = lax.all_gather(view_b, "row", axis=0, tiled=True)
    normed_a, scaled_a = normalize(whole_a)
    normed_b, scaled_b = normalize(whole_b)
    count = whole_a.shape[0]
    width_a = whole_a.shape[1]
    width_b = whole_b.shape[1]
    corr = (
        lax.dot_general(
            normed_a, normed_b, (((0,), (0,)), ((), ())), preferred_element_type=jnp.float32
        )
        / count
    )
    rows = lax.axis_index("row") * width_a + lax.iota(jnp.int32, width_a)
    columns = lax.axis_index("col") * width_b + lax.iota(jnp.int32, width_b)
    diag = rows[:, None] == columns[None, :]
    partial_loss = jnp.sum(jnp.where(diag, jnp.square(1.0 - corr), off_weight * jnp.square(corr)))
    weights = jnp.where(diag, 2.0 * (corr - 1.0), 2.0 * off_weight * corr).astype(jnp.bfloat16)
    term_a = lax.dot_general(
        normed_b, weights, (((1,), (1,)), ((), ())), preferred_element_type=jnp.float32
    )
    term_b = jnp.dot(normed_a, weights, preferred_element_type=jnp.float32)
    summed_a = lax.psum_scatter(term_a, "col", scatter_dimension=0, tiled=True)
    summed_b = lax.psum_scatter(term_b, "row", scatter_dimension=0, tiled=True)
    share_a = summed_a.shape[0]
    share_b = summed_b.shape[0]
    mine_a = lax.dynamic_slice_in_dim(normed_a, lax.axis_index("col") * share_a, share_a, 0).astype(
        jnp.float32
    )
    mine_b = lax.dynamic_slice_in_dim(normed_b, lax.axis_index("row") * share_b, share_b, 0).astype(
        jnp.float32
    )
    first_a, second_a = lax.psum((jnp.sum(summed_a, 0), jnp.sum(summed_a * mine_a, 0)), "col")
    first_b, second_b = lax.psum((jnp.sum(summed_b, 0), jnp.sum(summed_b * mine_b, 0)), "row")
    grad_a = (scaled_a * (summed_a - first_a / count - mine_a * (second_a / count))).astype(
        jnp.bfloat16
    )
    grad_b = (scaled_b * (summed_b - first_b / count - mine_b * (second_b / count))).astype(
        jnp.bfloat16
    )
    total = lax.psum(partial_loss, ("row", "col"))
    loss = total / (width_a * lax.axis_size("row"))
    return (loss, grad_a, grad_b)


def sibling(value, n_col):
    return lax.ppermute(value, "col", [(c, c ^ 1) for c in range(n_col)])


def flip(value, side, step):
    pairs = []
    for row in range(side):
        for z in range(side):
            pairs.append(((row * side + z) * 2, (row * side + (z ^ step)) * 2))
            pairs.append(((row * side + z) * 2 + 1, ((row ^ step) * side + z) * 2 + 1))
    return lax.ppermute(value, BOTH, pairs)


def across(value, side, step):
    pairs = []
    for row in range(side):
        for z in range(side):
            pairs.append(((row * side + z) * 2, ((row ^ step) * side + z) * 2))
            pairs.append(((row * side + z) * 2 + 1, (row * side + (z ^ step)) * 2 + 1))
    return lax.ppermute(value, BOTH, pairs)


def in_order(pieces, position):
    bit = 1
    while bit < len(pieces):
        on = (position & bit) != 0
        pieces = [jnp.where(on, pieces[i ^ bit], pieces[i]) for i in range(len(pieces))]
        bit *= 2
    return pieces


def rounded(value):
    return lax.reduce_precision(value, exponent_bits=8, mantissa_bits=7)


def split(value):
    high = rounded(value)
    return high.astype(jnp.bfloat16), rounded(value - high).astype(jnp.bfloat16)


def standardize(values):
    values = values.astype(jnp.float32)
    center = jnp.mean(values, 0)
    spread = jnp.mean(jnp.square(values - center), 0)
    scaled = lax.rsqrt(spread + epsilon)
    return (rounded((values - center) * scaled).astype(jnp.bfloat16), scaled)


def early(side):
    return [((v * side + v) * 2, ((v ^ 1) * side + (v ^ 1)) * 2) for v in range(side)]


def meetings(side):
    if side != 4:
        return None
    blocks = set(range(side))
    chips = [(row, z) for row in range(side) for z in range(side)]
    knows = {
        (row, z, core): {(z, row)[core]} | ({row ^ 1} if row == z and core == 0 else set())
        for row, z in chips
        for core in range(2)
    }

    def hops(p, q):
        return bin(p[0] ^ q[0]).count("1") + abs(p[1] - q[1])

    def search(choices, order, used):
        if not order:
            return []
        for tellers in choices[order[0]]:
            if not used & set(tellers):
                found = search(choices, order[1:], used | set(tellers))
                if found is not None:
                    return [(order[0], tellers)] + found
        return None

    for limit in range(1, 3 * side):
        choices = {}
        for chip in chips:
            own = knows[*chip, 0] | knows[*chip, 1]
            near = [d for d in knows if 0 < hops(d, chip) <= limit]
            tellers = [(d,) for d in near] + [(d, e) for i, d in enumerate(near) for e in near[i + 1 :]]
            choices[chip] = [t for t in tellers if own.union(*(knows[d] for d in t)) == blocks]
        if all(choices.values()):
            order = sorted(chips, key=lambda chip: len(choices[chip]))
            found = search(choices, order, set())
            if found:
                return [
                    ((d[0] * side + d[1]) * 2 + d[2], (chip[0] * side + chip[1]) * 2 + core)
                    for chip, tellers in found
                    for core, d in enumerate(tellers)
                ]
    return None


def gram_body(side, view_a, view_b):
    n_col = 2 * side
    share, width = view_a.shape
    pair, half = view_b.shape
    count = share * n_col
    row = lax.axis_index("row")
    col = lax.axis_index("col")
    z = lax.shift_right_logical(col, 1)
    is_a = (col & 1) == 0
    diagonal = row == z

    got_a, got_b = sibling(view_a, n_col), sibling(view_b, n_col)
    own = jnp.where(
        is_a, jnp.concatenate([view_a, got_a], 0), jnp.concatenate([got_b, view_b], 1)
    )

    pieces = [own] + [flip(own, side, step) for step in range(1, side)]
    mine = jnp.concatenate(in_order(pieces, jnp.where(is_a, z, row)), 0)
    other = sibling(mine, n_col)

    normed, scaled = standardize(mine)
    gram = lax.dot_general(
        normed, normed, (((1,), (1,)), ((), ())), preferred_element_type=jnp.float32
    )
    normed, gram, other = lax.optimization_barrier((normed, gram, other))
    other_normed, other_scaled = standardize(other)

    normed_f = normed.astype(jnp.float32)
    other_f = other_normed.astype(jnp.float32)
    corr = jnp.mean(normed_f * other_f, 0)
    slope = jnp.where(diagonal, rounded(2.0 * (corr - 1.0)) - 2.0 * off_weight * corr, 0.0)
    extra = (slope * (normed_f - jnp.mean(normed_f, 0) - other_f * corr)).astype(jnp.bfloat16)
    part = jnp.square(1.0 - corr) - off_weight * jnp.square(corr)
    part = jnp.sum(jnp.where(diagonal, part, 0.0).reshape(-1, 128), 0, keepdims=True)

    lanes = width // side

    def payload(images, gram, part):
        images = [images[:, i * lanes : (i + 1) * lanes] for i in range(side)]
        part = [jnp.broadcast_to(x, (count // 2, 128)) for x in split(part)]
        return jnp.concatenate([jnp.concatenate(images, 0), *split(gram), jnp.concatenate(part, 0)], 1)

    def images_of(step):
        return lax.dynamic_slice_in_dim(extra, (row ^ step) * pair, pair, 0)

    slots = lax.broadcasted_iota(jnp.int32, (2 * side, 128), 0)

    def in_slot(part, block):
        return jnp.where((slots & (side - 1)) == block, jnp.where(slots < side, part, 1.0), 0.0)

    plan = meetings(side)
    landed = [payload(images_of(0), gram, part)]
    landed += [across(payload(images_of(step), gram, part), side, step) for step in range(1, side)]
    told = 0.0
    if plan:
        told = lax.ppermute(jnp.where(diagonal, in_slot(part, row), 0.0), BOTH, early(side))
    summed = sum(x.astype(jnp.float32) for x in landed)
    gram = summed[:, lanes : lanes + count] + summed[:, lanes + count : lanes + 2 * count]
    part = summed[:1, lanes + 2 * count :] + summed[count // 2 : count // 2 + 1, lanes + 2 * count :]

    sent = jnp.concatenate([summed[:, :lanes].astype(jnp.bfloat16), *split(gram)], 1)
    came = sibling(sent, n_col)
    for_a = jnp.where(is_a, came, sent)
    for_b = jnp.where(is_a, sent, came)

    known = in_slot(part, jnp.where(is_a, z, row)) + told
    heard = jnp.zeros_like(known)
    if plan:
        heard = lax.ppermute(known, BOTH, plan)
    else:
        known = jnp.where(is_a, known, 0.0)
        step = 1
        while step < side:
            known = known + lax.ppermute(known, "col", [(c, c ^ (2 * step)) for c in range(n_col)])
            step *= 2

    twice = [jnp.where(is_a, normed, other_normed)] * 2
    all_a = jnp.concatenate(twice, 0)
    twice = [jnp.where(is_a, other_normed[:, :half], normed[:, half:])] * 2
    all_b = jnp.concatenate(twice, 0)
    scaled_a = jnp.where(is_a, scaled, other_scaled)
    scaled_b = jnp.where(is_a, other_scaled[:half], scaled[half:])

    def images_in(sums):
        return jnp.concatenate([sums[i * pair : (i + 1) * pair, :lanes] for i in range(side)], 1)

    extra_a = images_in(for_a)
    extra_a = jnp.where(is_a, extra_a[:share], extra_a[share:])
    extra_b = images_in(for_b)
    extra_b = jnp.where(is_a, extra_b[:, :half], extra_b[:, half:])

    def terms(sums, twice):
        halves = sums[:, lanes : lanes + 2 * count]
        term = jnp.dot(halves, twice, preferred_element_type=jnp.float32)
        term = term * (2.0 * off_weight / count)
        return (term, jnp.mean(term, 0), jnp.mean(term * twice[:count].astype(jnp.float32), 0))

    def gradient(terms, twice, scaled, extra, start, images):
        term, first, second = terms
        term = lax.dynamic_slice_in_dim(term, start, images, 0)
        normed = lax.dynamic_slice_in_dim(twice, start, images, 0).astype(jnp.float32)
        return (scaled * (term - first - normed * second + extra.astype(jnp.float32))).astype(
            jnp.bfloat16
        )

    def whole(sums):
        sums = sums.astype(jnp.float32)
        return sums[:, lanes : lanes + count] + sums[:, lanes + count : lanes + 2 * count]

    everywhere = whole(for_a) * whole(for_b) * (off_weight / (count * count * width * side))
    everywhere = jnp.pad(jnp.sum(everywhere, 0), (0, 128 - count))
    terms_a, terms_b = terms(for_a, all_a), terms(for_b, all_b)
    heard, terms_a, terms_b, everywhere = lax.optimization_barrier(
        (heard, terms_a, terms_b, everywhere)
    )
    known = known + heard
    known = known + sibling(known, n_col)
    grad_a = gradient(terms_a, all_a, scaled_a, extra_a, col * share, share)
    grad_b = gradient(terms_b, all_b, scaled_b, extra_b, row * pair, pair)
    on_diagonal = known[:side] * (1.0 / (width * side)) / known[side:]
    loss = jnp.sum(everywhere + jnp.sum(on_diagonal, 0))
    return (loss, grad_a, grad_b)


def solution(mesh):
    in_specs = (P("col", "row"), P("row", "col"))
    out_specs = (P(), P("col", "row"), P("row", "col"))
    n_row, n_col = mesh.shape["row"], mesh.shape["col"]
    square = n_col == 2 * n_row and n_row & (n_row - 1) == 0

    def body(view_a, view_b):
        share, width = view_a.shape
        count = share * n_col
        fits = view_b.shape == (2 * share, width // 2) and width % (128 * n_row) == 0
        fits = fits and share % 8 == 0 and count <= 128 and 2 * count % 128 == 0
        if square and fits:
            return gram_body(n_row, view_a, view_b)
        return tiled_body(view_a, view_b)

    return jax.shard_map(body, mesh=mesh, in_specs=in_specs, out_specs=out_specs, check_vma=False)
```

```python
import jax
import jax.numpy as jnp
from jax import lax
from jax.sharding import PartitionSpec as P

off_weight = 0.0051
epsilon = 1e-05

BOTH = ("row", "col")


def normalize(values):
    values = values.astype(jnp.float32)
    center = jnp.mean(values, 0)
    spread = jnp.mean(jnp.square(values - center), 0)
    scaled = lax.rsqrt(spread + epsilon)
    return (((values - center) * scaled).astype(jnp.bfloat16), scaled)


def tiled_body(view_a, view_b):
    whole_a = lax.all_gather(view_a, "col", axis=0, tiled=True)
    whole_b = lax.all_gather(view_b, "row", axis=0, tiled=True)
    normed_a, scaled_a = normalize(whole_a)
    normed_b, scaled_b = normalize(whole_b)
    count = whole_a.shape[0]
    width_a = whole_a.shape[1]
    width_b = whole_b.shape[1]
    corr = (
        lax.dot_general(
            normed_a, normed_b, (((0,), (0,)), ((), ())), preferred_element_type=jnp.float32
        )
        / count
    )
    rows = lax.axis_index("row") * width_a + lax.iota(jnp.int32, width_a)
    columns = lax.axis_index("col") * width_b + lax.iota(jnp.int32, width_b)
    diag = rows[:, None] == columns[None, :]
    partial_loss = jnp.sum(jnp.where(diag, jnp.square(1.0 - corr), off_weight * jnp.square(corr)))
    weights = jnp.where(diag, 2.0 * (corr - 1.0), 2.0 * off_weight * corr).astype(jnp.bfloat16)
    term_a = lax.dot_general(
        normed_b, weights, (((1,), (1,)), ((), ())), preferred_element_type=jnp.float32
    )
    term_b = jnp.dot(normed_a, weights, preferred_element_type=jnp.float32)
    summed_a = lax.psum_scatter(term_a, "col", scatter_dimension=0, tiled=True)
    summed_b = lax.psum_scatter(term_b, "row", scatter_dimension=0, tiled=True)
    share_a = summed_a.shape[0]
    share_b = summed_b.shape[0]
    mine_a = lax.dynamic_slice_in_dim(normed_a, lax.axis_index("col") * share_a, share_a, 0).astype(
        jnp.float32
    )
    mine_b = lax.dynamic_slice_in_dim(normed_b, lax.axis_index("row") * share_b, share_b, 0).astype(
        jnp.float32
    )
    first_a, second_a = lax.psum((jnp.sum(summed_a, 0), jnp.sum(summed_a * mine_a, 0)), "col")
    first_b, second_b = lax.psum((jnp.sum(summed_b, 0), jnp.sum(summed_b * mine_b, 0)), "row")
    grad_a = (scaled_a * (summed_a - first_a / count - mine_a * (second_a / count))).astype(
        jnp.bfloat16
    )
    grad_b = (scaled_b * (summed_b - first_b / count - mine_b * (second_b / count))).astype(
        jnp.bfloat16
    )
    total = lax.psum(partial_loss, ("row", "col"))
    loss = total / (width_a * lax.axis_size("row"))
    return (loss, grad_a, grad_b)


def sibling(value, n_col):
    return lax.ppermute(value, "col", [(c, c ^ 1) for c in range(n_col)])


def flip(value, side, step):
    pairs = []
    for row in range(side):
        for z in range(side):
            pairs.append(((row * side + z) * 2, (row * side + (z ^ step)) * 2))
            pairs.append(((row * side + z) * 2 + 1, ((row ^ step) * side + z) * 2 + 1))
    return lax.ppermute(value, BOTH, pairs)


def across(value, side, step):
    pairs = []
    for row in range(side):
        for z in range(side):
            pairs.append(((row * side + z) * 2, ((row ^ step) * side + z) * 2))
            pairs.append(((row * side + z) * 2 + 1, (row * side + (z ^ step)) * 2 + 1))
    return lax.ppermute(value, BOTH, pairs)


def in_order(pieces, position):
    bit = 1
    while bit < len(pieces):
        on = (position & bit) != 0
        pieces = [jnp.where(on, pieces[i ^ bit], pieces[i]) for i in range(len(pieces))]
        bit *= 2
    return pieces


def rounded(value):
    return lax.reduce_precision(value, exponent_bits=8, mantissa_bits=7)


def split(value):
    high = rounded(value)
    return high.astype(jnp.bfloat16), rounded(value - high).astype(jnp.bfloat16)


def standardize(values):
    values = values.astype(jnp.float32)
    center = jnp.mean(values, 0)
    spread = jnp.mean(jnp.square(values - center), 0)
    scaled = lax.rsqrt(spread + epsilon)
    return (rounded((values - center) * scaled).astype(jnp.bfloat16), scaled)


def meetings(side):
    chips = [(row, z) for row in range(side) for z in range(side)]

    def hops(p, q):
        return bin(p[0] ^ q[0]).count("1") + abs(p[1] - q[1])

    def search(choices, order, used, chosen):
        if len(chosen) == len(order):
            return dict(chosen)
        chip = order[len(chosen)]
        for pair in choices[chip]:
            if all(used[q] < 2 for q in pair):
                for q in pair:
                    used[q] += 1
                found = search(choices, order, used, chosen + [(chip, pair)])
                if found:
                    return found
                for q in pair:
                    used[q] -= 1
        return None

    if side > 6:
        return None
    for limit in range(1, 3 * side):
        choices = {
            p: [
                (q, t)
                for i, q in enumerate(chips)
                for t in chips[i + 1 :]
                if max(hops(p, q), hops(p, t)) <= limit and len({*p, *q, *t}) == side
            ]
            for p in chips
        }
        if all(choices.values()):
            order = sorted(chips, key=lambda p: len(choices[p]))
            found = search(choices, order, dict.fromkeys(chips, 0), [])
            if found:
                return found
    return None


def joined(known, heard):
    side = known.shape[0] // 2
    here = known[side:] > 0.0
    return jnp.concatenate(
        [jnp.where(here, known[:side], heard[:side]), jnp.maximum(known[side:], heard[side:])], 0
    )


def total(values):
    while len(values) > 1:
        values = [x + y for x, y in zip(values[::2], values[1::2])]
    return values[0]


def hear(known, side):
    plan = meetings(side)
    used, pairs = {}, []
    for (row, z), pair in plan.items():
        for core, chip in enumerate(pair):
            from_core = used.get(chip, 0)
            used[chip] = from_core + 1
            pairs.append(((chip[0] * side + chip[1]) * 2 + from_core, (row * side + z) * 2 + core))
    return lax.ppermute(known, BOTH, pairs)


def gram_body(side, view_a, view_b):
    n_col = 2 * side
    share, width = view_a.shape
    pair, half = view_b.shape
    count = share * n_col
    row = lax.axis_index("row")
    col = lax.axis_index("col")
    z = lax.shift_right_logical(col, 1)
    is_a = (col & 1) == 0
    diagonal = row == z

    got_a, got_b = sibling(view_a, n_col), sibling(view_b, n_col)
    own = jnp.where(
        is_a, jnp.concatenate([view_a, got_a], 0), jnp.concatenate([got_b, view_b], 1)
    )

    pieces = {step: flip(own, side, step) for step in range(1, side)}
    pieces = [own] + [pieces[step] for step in range(1, side)]
    mine = jnp.concatenate(in_order(pieces, jnp.where(is_a, z, row)), 0)
    other = sibling(mine, n_col)

    normed, scaled = standardize(mine)
    gram = lax.dot_general(
        normed, normed, (((1,), (1,)), ((), ())), preferred_element_type=jnp.float32
    )
    normed, gram, other = lax.optimization_barrier((normed, gram, other))
    other_normed, other_scaled = standardize(other)

    normed_f = normed.astype(jnp.float32)
    other_f = other_normed.astype(jnp.float32)
    corr = jnp.mean(normed_f * other_f, 0)
    slope = jnp.where(diagonal, rounded(2.0 * (corr - 1.0)) - 2.0 * off_weight * corr, 0.0)
    extra = (slope * (normed_f - jnp.mean(normed_f, 0) - other_f * corr)).astype(jnp.bfloat16)
    part = jnp.square(1.0 - corr) - off_weight * jnp.square(corr)
    part = jnp.sum(jnp.where(diagonal, part, 0.0).reshape(-1, 128), 0, keepdims=True)

    lanes = width // side

    def payload(images, gram, part):
        images = [images[:, i * lanes : (i + 1) * lanes] for i in range(side)]
        part = [jnp.broadcast_to(x, (count // 2, 128)) for x in split(part)]
        return jnp.concatenate([jnp.concatenate(images, 0), *split(gram), jnp.concatenate(part, 0)], 1)

    def images_of(step):
        return lax.dynamic_slice_in_dim(extra, (row ^ step) * pair, pair, 0)

    landed = {step: across(payload(images_of(step), gram, part), side, step) for step in range(1, side)}
    landed[0] = payload(images_of(0), gram, part)
    summed = total([landed[step].astype(jnp.float32) for step in range(side)])
    gram = summed[:, lanes : lanes + count] + summed[:, lanes + count : lanes + 2 * count]
    part = summed[:1, lanes + 2 * count :] + summed[count // 2 : count // 2 + 1, lanes + 2 * count :]

    sent = jnp.concatenate([summed[:, :lanes].astype(jnp.bfloat16), *split(gram)], 1)
    came = sibling(sent, n_col)
    for_a = jnp.where(is_a, came, sent)
    for_b = jnp.where(is_a, sent, came)

    slots = lax.broadcasted_iota(jnp.int32, (2 * side, 128), 0)
    known = jnp.where(slots < side, part, 1.0)
    known = jnp.where((slots & (side - 1)) == jnp.where(is_a, z, row), known, 0.0)
    known = joined(known, sibling(known, n_col))
    heard = hear(known, side)

    twice = [jnp.where(is_a, normed, other_normed)] * 2
    all_a = jnp.concatenate(twice, 0)
    twice = [jnp.where(is_a, other_normed[:, :half], normed[:, half:])] * 2
    all_b = jnp.concatenate(twice, 0)
    scaled_a = jnp.where(is_a, scaled, other_scaled)
    scaled_b = jnp.where(is_a, other_scaled[:half], scaled[half:])

    def images_in(sums):
        return jnp.concatenate([sums[i * pair : (i + 1) * pair, :lanes] for i in range(side)], 1)

    extra_a = images_in(for_a)
    extra_a = jnp.where(is_a, extra_a[:share], extra_a[share:])
    extra_b = images_in(for_b)
    extra_b = jnp.where(is_a, extra_b[:, :half], extra_b[:, half:])

    def terms(sums, twice):
        halves = sums[:, lanes : lanes + 2 * count]
        term = jnp.dot(halves, twice, preferred_element_type=jnp.float32)
        term = term * (2.0 * off_weight / count)
        return (term, jnp.mean(term, 0), jnp.mean(term * twice[:count].astype(jnp.float32), 0))

    def gradient(terms, twice, scaled, extra, start, images):
        term, first, second = terms
        term = lax.dynamic_slice_in_dim(term, start, images, 0)
        normed = lax.dynamic_slice_in_dim(twice, start, images, 0).astype(jnp.float32)
        return (scaled * (term - first - normed * second + extra.astype(jnp.float32))).astype(
            jnp.bfloat16
        )

    def whole(sums):
        sums = sums.astype(jnp.float32)
        return sums[:, lanes : lanes + count] + sums[:, lanes + count : lanes + 2 * count]

    everywhere = whole(for_a) * whole(for_b) * (off_weight / (count * count * width * side))
    everywhere = jnp.pad(jnp.sum(everywhere, 0), (0, 128 - count))
    grad_a = gradient(terms(for_a, all_a), all_a, scaled_a, extra_a, col * share, share)
    grad_b = gradient(terms(for_b, all_b), all_b, scaled_b, extra_b, row * pair, pair)

    heard, grad_a, grad_b, everywhere = lax.optimization_barrier((heard, grad_a, grad_b, everywhere))
    known = joined(known, heard)
    known = joined(known, sibling(known, n_col))
    loss = jnp.sum(everywhere + jnp.sum(known[:side], 0) * (1.0 / (width * side)))
    return (loss, grad_a, grad_b)


def solution(mesh):
    in_specs = (P("col", "row"), P("row", "col"))
    out_specs = (P(), P("col", "row"), P("row", "col"))
    n_row, n_col = mesh.shape["row"], mesh.shape["col"]
    square = n_col == 2 * n_row and n_row & (n_row - 1) == 0

    def body(view_a, view_b):
        share, width = view_a.shape
        count = share * n_col
        fits = view_b.shape == (2 * share, width // 2) and width % (128 * n_row) == 0
        fits = fits and share % 8 == 0 and count <= 128 and 2 * count % 128 == 0
        if square and fits and meetings(n_row):
            return gram_body(n_row, view_a, view_b)
        return tiled_body(view_a, view_b)

    return jax.shard_map(body, mesh=mesh, in_specs=in_specs, out_specs=out_specs, check_vma=False)
```

```python
import jax
import jax.numpy as jnp
from jax import lax
from jax.sharding import PartitionSpec as P

off_weight = 0.0051
epsilon = 1e-05

BOTH = ("row", "col")


def normalize(values):
    values = values.astype(jnp.float32)
    center = jnp.mean(values, 0)
    spread = jnp.mean(jnp.square(values - center), 0)
    scaled = lax.rsqrt(spread + epsilon)
    return (((values - center) * scaled).astype(jnp.bfloat16), scaled)


def tiled_body(view_a, view_b):
    whole_a = lax.all_gather(view_a, "col", axis=0, tiled=True)
    whole_b = lax.all_gather(view_b, "row", axis=0, tiled=True)
    normed_a, scaled_a = normalize(whole_a)
    normed_b, scaled_b = normalize(whole_b)
    count = whole_a.shape[0]
    width_a = whole_a.shape[1]
    width_b = whole_b.shape[1]
    corr = (
        lax.dot_general(
            normed_a, normed_b, (((0,), (0,)), ((), ())), preferred_element_type=jnp.float32
        )
        / count
    )
    rows = lax.axis_index("row") * width_a + lax.iota(jnp.int32, width_a)
    columns = lax.axis_index("col") * width_b + lax.iota(jnp.int32, width_b)
    diag = rows[:, None] == columns[None, :]
    partial_loss = jnp.sum(jnp.where(diag, jnp.square(1.0 - corr), off_weight * jnp.square(corr)))
    weights = jnp.where(diag, 2.0 * (corr - 1.0), 2.0 * off_weight * corr).astype(jnp.bfloat16)
    term_a = lax.dot_general(
        normed_b, weights, (((1,), (1,)), ((), ())), preferred_element_type=jnp.float32
    )
    term_b = jnp.dot(normed_a, weights, preferred_element_type=jnp.float32)
    summed_a = lax.psum_scatter(term_a, "col", scatter_dimension=0, tiled=True)
    summed_b = lax.psum_scatter(term_b, "row", scatter_dimension=0, tiled=True)
    share_a = summed_a.shape[0]
    share_b = summed_b.shape[0]
    mine_a = lax.dynamic_slice_in_dim(normed_a, lax.axis_index("col") * share_a, share_a, 0).astype(
        jnp.float32
    )
    mine_b = lax.dynamic_slice_in_dim(normed_b, lax.axis_index("row") * share_b, share_b, 0).astype(
        jnp.float32
    )
    first_a, second_a = lax.psum((jnp.sum(summed_a, 0), jnp.sum(summed_a * mine_a, 0)), "col")
    first_b, second_b = lax.psum((jnp.sum(summed_b, 0), jnp.sum(summed_b * mine_b, 0)), "row")
    grad_a = (scaled_a * (summed_a - first_a / count - mine_a * (second_a / count))).astype(
        jnp.bfloat16
    )
    grad_b = (scaled_b * (summed_b - first_b / count - mine_b * (second_b / count))).astype(
        jnp.bfloat16
    )
    total = lax.psum(partial_loss, ("row", "col"))
    loss = total / (width_a * lax.axis_size("row"))
    return (loss, grad_a, grad_b)


def sibling(value, n_col):
    return lax.ppermute(value, "col", [(c, c ^ 1) for c in range(n_col)])


def flip(value, side, step):
    pairs = []
    for row in range(side):
        for z in range(side):
            pairs.append(((row * side + z) * 2, (row * side + (z ^ step)) * 2))
            pairs.append(((row * side + z) * 2 + 1, ((row ^ step) * side + z) * 2 + 1))
    return lax.ppermute(value, BOTH, pairs)


def across(value, side, step, along_z=1):
    pairs = []
    for row in range(side):
        for z in range(side):
            for core in range(2):
                to = (row, z ^ step) if core == along_z else (row ^ step, z)
                pairs.append(((row * side + z) * 2 + core, (to[0] * side + to[1]) * 2 + core))
    return lax.ppermute(value, BOTH, pairs)


def in_order(pieces, position):
    bit = 1
    while bit < len(pieces):
        on = (position & bit) != 0
        pieces = [jnp.where(on, pieces[i ^ bit], pieces[i]) for i in range(len(pieces))]
        bit *= 2
    return pieces


def rounded(value):
    return lax.reduce_precision(value, exponent_bits=8, mantissa_bits=7)


def split(value):
    high = rounded(value)
    return high.astype(jnp.bfloat16), rounded(value - high).astype(jnp.bfloat16)


def standardize(values):
    values = values.astype(jnp.float32)
    center = jnp.mean(values, 0)
    spread = jnp.mean(jnp.square(values - center), 0)
    scaled = lax.rsqrt(spread + epsilon)
    return (rounded((values - center) * scaled).astype(jnp.bfloat16), scaled)


def meetings(side):
    chips = [(row, z) for row in range(side) for z in range(side)]

    def hops(p, q):
        return bin(p[0] ^ q[0]).count("1") + abs(p[1] - q[1])

    def search(choices, order, used, chosen):
        if len(chosen) == len(order):
            return dict(chosen)
        chip = order[len(chosen)]
        for pair in choices[chip]:
            if all(used[q] < 2 for q in pair):
                for q in pair:
                    used[q] += 1
                found = search(choices, order, used, chosen + [(chip, pair)])
                if found:
                    return found
                for q in pair:
                    used[q] -= 1
        return None

    if side > 6:
        return None
    for limit in range(1, 3 * side):
        choices = {
            p: [
                (q, t)
                for i, q in enumerate(chips)
                for t in chips[i + 1 :]
                if max(hops(p, q), hops(p, t)) <= limit and len({*p, *q, *t}) == side
            ]
            for p in chips
        }
        if all(choices.values()):
            order = sorted(chips, key=lambda p: len(choices[p]))
            found = search(choices, order, dict.fromkeys(chips, 0), [])
            if found:
                return found
    return None


def joined(known, heard):
    side = known.shape[0] // 2
    here = known[side:] > 0.0
    return jnp.concatenate(
        [jnp.where(here, known[:side], heard[:side]), jnp.maximum(known[side:], heard[side:])], 0
    )


def total(values):
    while len(values) > 1:
        values = [x + y for x, y in zip(values[::2], values[1::2])]
    return values[0]


def hear(known, side):
    plan = meetings(side)
    used, pairs = {}, []
    for (row, z), pair in plan.items():
        for core, chip in enumerate(pair):
            from_core = used.get(chip, 0)
            used[chip] = from_core + 1
            pairs.append(((chip[0] * side + chip[1]) * 2 + from_core, (row * side + z) * 2 + core))
    return lax.ppermute(known, BOTH, pairs)


def gram_body(side, view_a, view_b):
    n_col = 2 * side
    share, width = view_a.shape
    pair, half = view_b.shape
    count = share * n_col
    row = lax.axis_index("row")
    col = lax.axis_index("col")
    z = lax.shift_right_logical(col, 1)
    is_a = (col & 1) == 0
    diagonal = row == z

    got_a, got_b = sibling(view_a, n_col), sibling(view_b, n_col)
    own = jnp.where(
        is_a, jnp.concatenate([view_a, got_a], 0), jnp.concatenate([got_b, view_b], 1)
    )

    pieces = {step: flip(own, side, step) for step in range(1, side)}
    pieces = [own] + [pieces[step] for step in range(1, side)]
    mine = jnp.concatenate(in_order(pieces, jnp.where(is_a, z, row)), 0)
    other = sibling(mine, n_col)

    normed, scaled = standardize(mine)
    gram = lax.dot_general(
        normed, normed, (((1,), (1,)), ((), ())), preferred_element_type=jnp.float32
    )
    normed, gram, other = lax.optimization_barrier((normed, gram, other))
    other_normed, other_scaled = standardize(other)

    normed_f = normed.astype(jnp.float32)
    other_f = other_normed.astype(jnp.float32)
    corr = jnp.mean(normed_f * other_f, 0)
    slope = jnp.where(diagonal, rounded(2.0 * (corr - 1.0)) - 2.0 * off_weight * corr, 0.0)
    extra = (slope * (normed_f - jnp.mean(normed_f, 0) - other_f * corr)).astype(jnp.bfloat16)
    other_extra = (slope * (other_f - jnp.mean(other_f, 0) - normed_f * corr)).astype(jnp.bfloat16)
    other_gram = lax.dot_general(
        other_normed, other_normed, (((1,), (1,)), ((), ())), preferred_element_type=jnp.float32
    )
    part = jnp.square(1.0 - corr) - off_weight * jnp.square(corr)
    part = jnp.sum(jnp.where(diagonal, part, 0.0).reshape(-1, 128), 0, keepdims=True)

    lanes = width // side

    def payload(images, gram, part):
        images = [images[:, i * lanes : (i + 1) * lanes] for i in range(side)]
        part = [jnp.broadcast_to(x, (count // 2, 128)) for x in split(part)]
        return jnp.concatenate([jnp.concatenate(images, 0), *split(gram), jnp.concatenate(part, 0)], 1)

    def images_of(extra, step):
        return lax.dynamic_slice_in_dim(extra, (row ^ step) * pair, pair, 0)

    changed = 3
    landed = {}
    for step in [1, 2, 3]:
        if step == changed:
            lone = across(payload(images_of(other_extra, step), other_gram, part), side, step, 0)
        else:
            landed[step] = across(payload(images_of(extra, step), gram, part), side, step, 1)
    landed[0] = payload(images_of(extra, 0), gram, part)

    def section(value, i):
        first = (0, lanes, lanes + 2 * count, lanes + 2 * count + 128)
        return value[:, first[i] : first[i + 1]].astype(jnp.float32)

    def whole(halves):
        return halves[:, :count] + halves[:, count:]

    def part_of(value):
        value = section(value, 2)
        return value[:1] + value[count // 2 : count // 2 + 1]

    slots = lax.broadcasted_iota(jnp.int32, (2 * side, 128), 0)
    at = jnp.where(jnp.logical_xor(is_a, (row ^ z) == changed), z, row)
    known = jnp.where(slots < side, part_of(lone) + sum(part_of(landed[i]) for i in landed), 1.0)
    known = jnp.where((slots & (side - 1)) == at, known, 0.0)
    known = joined(known, sibling(known, n_col))
    heard = hear(known, side)

    near = landed[changed ^ 1]
    far = total([whole(section(landed[i], 1)) for i in landed if i != changed ^ 1])
    images = sum(section(landed[i], 0) for i in landed).astype(jnp.bfloat16)
    sent = jnp.concatenate([images, near[:, lanes : lanes + 2 * count], *split(far)], 1)
    came = sibling(sent, n_col)
    lone_came = sibling(lone[:, : lanes + 2 * count], n_col)

    def sums_of(most, lone):
        gram = whole(section(most, 1)) + whole(section(lone, 1)) + whole(section(most, 2))
        images = (section(most, 0) + section(lone, 0)).astype(jnp.bfloat16)
        return jnp.concatenate([images, *split(gram)], 1)

    for_a = sums_of(jnp.where(is_a, came, sent), jnp.where(is_a, lone[:, : lanes + 2 * count], lone_came))
    for_b = sums_of(jnp.where(is_a, sent, came), jnp.where(is_a, lone_came, lone[:, : lanes + 2 * count]))

    twice = [jnp.where(is_a, normed, other_normed)] * 2
    all_a = jnp.concatenate(twice, 0)
    twice = [jnp.where(is_a, other_normed[:, :half], normed[:, half:])] * 2
    all_b = jnp.concatenate(twice, 0)
    scaled_a = jnp.where(is_a, scaled, other_scaled)
    scaled_b = jnp.where(is_a, other_scaled[:half], scaled[half:])

    def images_in(sums):
        return jnp.concatenate([sums[i * pair : (i + 1) * pair, :lanes] for i in range(side)], 1)

    extra_a = images_in(for_a)
    extra_a = jnp.where(is_a, extra_a[:share], extra_a[share:])
    extra_b = images_in(for_b)
    extra_b = jnp.where(is_a, extra_b[:, :half], extra_b[:, half:])

    def terms(sums, twice):
        halves = sums[:, lanes : lanes + 2 * count]
        term = jnp.dot(halves, twice, preferred_element_type=jnp.float32)
        term = term * (2.0 * off_weight / count)
        return (term, jnp.mean(term, 0), jnp.mean(term * twice[:count].astype(jnp.float32), 0))

    def gradient(terms, twice, scaled, extra, start, images):
        term, first, second = terms
        term = lax.dynamic_slice_in_dim(term, start, images, 0)
        normed = lax.dynamic_slice_in_dim(twice, start, images, 0).astype(jnp.float32)
        return (scaled * (term - first - normed * second + extra.astype(jnp.float32))).astype(
            jnp.bfloat16
        )

    everywhere = whole(section(for_a, 1)) * whole(section(for_b, 1))
    everywhere = everywhere * (off_weight / (count * count * width * side))
    everywhere = jnp.pad(jnp.sum(everywhere, 0), (0, 128 - count))
    grad_a = gradient(terms(for_a, all_a), all_a, scaled_a, extra_a, col * share, share)
    grad_b = gradient(terms(for_b, all_b), all_b, scaled_b, extra_b, row * pair, pair)

    heard, grad_a, grad_b, everywhere = lax.optimization_barrier((heard, grad_a, grad_b, everywhere))
    known = joined(known, heard)
    known = joined(known, sibling(known, n_col))
    loss = jnp.sum(everywhere + jnp.sum(known[:side], 0) * (1.0 / (width * side)))
    return (loss, grad_a, grad_b)


def solution(mesh):
    in_specs = (P("col", "row"), P("row", "col"))
    out_specs = (P(), P("col", "row"), P("row", "col"))
    n_row, n_col = mesh.shape["row"], mesh.shape["col"]
    square = n_col == 2 * n_row and n_row & (n_row - 1) == 0

    def body(view_a, view_b):
        share, width = view_a.shape
        count = share * n_col
        fits = view_b.shape == (2 * share, width // 2) and width % (128 * n_row) == 0
        fits = fits and share % 8 == 0 and count <= 128 and 2 * count % 128 == 0
        if square and fits and meetings(n_row):
            return gram_body(n_row, view_a, view_b)
        return tiled_body(view_a, view_b)

    return jax.shard_map(body, mesh=mesh, in_specs=in_specs, out_specs=out_specs, check_vma=False)
```

```python
import jax
import jax.numpy as jnp
from jax import lax
from jax.sharding import PartitionSpec as P

off_weight = 0.0051
epsilon = 1e-05

BOTH = ("row", "col")


def normalize(values):
    values = values.astype(jnp.float32)
    center = jnp.mean(values, 0)
    spread = jnp.mean(jnp.square(values - center), 0)
    scaled = lax.rsqrt(spread + epsilon)
    return (((values - center) * scaled).astype(jnp.bfloat16), scaled)


def tiled_body(view_a, view_b):
    whole_a = lax.all_gather(view_a, "col", axis=0, tiled=True)
    whole_b = lax.all_gather(view_b, "row", axis=0, tiled=True)
    normed_a, scaled_a = normalize(whole_a)
    normed_b, scaled_b = normalize(whole_b)
    count = whole_a.shape[0]
    width_a = whole_a.shape[1]
    width_b = whole_b.shape[1]
    corr = (
        lax.dot_general(
            normed_a, normed_b, (((0,), (0,)), ((), ())), preferred_element_type=jnp.float32
        )
        / count
    )
    rows = lax.axis_index("row") * width_a + lax.iota(jnp.int32, width_a)
    columns = lax.axis_index("col") * width_b + lax.iota(jnp.int32, width_b)
    diag = rows[:, None] == columns[None, :]
    partial_loss = jnp.sum(jnp.where(diag, jnp.square(1.0 - corr), off_weight * jnp.square(corr)))
    weights = jnp.where(diag, 2.0 * (corr - 1.0), 2.0 * off_weight * corr).astype(jnp.bfloat16)
    term_a = lax.dot_general(
        normed_b, weights, (((1,), (1,)), ((), ())), preferred_element_type=jnp.float32
    )
    term_b = jnp.dot(normed_a, weights, preferred_element_type=jnp.float32)
    summed_a = lax.psum_scatter(term_a, "col", scatter_dimension=0, tiled=True)
    summed_b = lax.psum_scatter(term_b, "row", scatter_dimension=0, tiled=True)
    share_a = summed_a.shape[0]
    share_b = summed_b.shape[0]
    mine_a = lax.dynamic_slice_in_dim(normed_a, lax.axis_index("col") * share_a, share_a, 0).astype(
        jnp.float32
    )
    mine_b = lax.dynamic_slice_in_dim(normed_b, lax.axis_index("row") * share_b, share_b, 0).astype(
        jnp.float32
    )
    first_a, second_a = lax.psum((jnp.sum(summed_a, 0), jnp.sum(summed_a * mine_a, 0)), "col")
    first_b, second_b = lax.psum((jnp.sum(summed_b, 0), jnp.sum(summed_b * mine_b, 0)), "row")
    grad_a = (scaled_a * (summed_a - first_a / count - mine_a * (second_a / count))).astype(
        jnp.bfloat16
    )
    grad_b = (scaled_b * (summed_b - first_b / count - mine_b * (second_b / count))).astype(
        jnp.bfloat16
    )
    total = lax.psum(partial_loss, ("row", "col"))
    loss = total / (width_a * lax.axis_size("row"))
    return (loss, grad_a, grad_b)


def sibling(value, n_col):
    return lax.ppermute(value, "col", [(c, c ^ 1) for c in range(n_col)])


def flip(value, side, step):
    pairs = []
    for row in range(side):
        for z in range(side):
            pairs.append(((row * side + z) * 2, (row * side + (z ^ step)) * 2))
            pairs.append(((row * side + z) * 2 + 1, ((row ^ step) * side + z) * 2 + 1))
    return lax.ppermute(value, BOTH, pairs)


def across(value, side, step):
    pairs = []
    for row in range(side):
        for z in range(side):
            pairs.append(((row * side + z) * 2, ((row ^ step) * side + z) * 2))
            pairs.append(((row * side + z) * 2 + 1, (row * side + (z ^ step)) * 2 + 1))
    return lax.ppermute(value, BOTH, pairs)


def in_order(pieces, position):
    bit = 1
    while bit < len(pieces):
        on = (position & bit) != 0
        pieces = [jnp.where(on, pieces[i ^ bit], pieces[i]) for i in range(len(pieces))]
        bit *= 2
    return pieces


def rounded(value):
    return lax.reduce_precision(value, exponent_bits=8, mantissa_bits=7)


def split(value):
    high = rounded(value)
    return high.astype(jnp.bfloat16), rounded(value - high).astype(jnp.bfloat16)


def standardize(values):
    values = values.astype(jnp.float32)
    center = jnp.mean(values, 0)
    spread = jnp.mean(jnp.square(values - center), 0)
    scaled = lax.rsqrt(spread + epsilon)
    return (rounded((values - center) * scaled).astype(jnp.bfloat16), scaled)


def meetings(side):
    chips = [(row, z) for row in range(side) for z in range(side)]

    def hops(p, q):
        return bin(p[0] ^ q[0]).count("1") + abs(p[1] - q[1])

    def search(choices, order, used, chosen):
        if len(chosen) == len(order):
            return dict(chosen)
        chip = order[len(chosen)]
        for pair in choices[chip]:
            if all(used[q] < 2 for q in pair):
                for q in pair:
                    used[q] += 1
                found = search(choices, order, used, chosen + [(chip, pair)])
                if found:
                    return found
                for q in pair:
                    used[q] -= 1
        return None

    if side > 6:
        return None
    for limit in range(1, 3 * side):
        choices = {
            p: [
                (q, t)
                for i, q in enumerate(chips)
                for t in chips[i + 1 :]
                if max(hops(p, q), hops(p, t)) <= limit and len({*p, *q, *t}) == side
            ]
            for p in chips
        }
        if all(choices.values()):
            order = sorted(chips, key=lambda p: len(choices[p]))
            found = search(choices, order, dict.fromkeys(chips, 0), [])
            if found:
                return found
    return None


def joined(known, heard):
    side = known.shape[0] // 2
    here = known[side:] > 0.0
    return jnp.concatenate(
        [jnp.where(here, known[:side], heard[:side]), jnp.maximum(known[side:], heard[side:])], 0
    )


def total(values):
    while len(values) > 1:
        values = [x + y for x, y in zip(values[::2], values[1::2])]
    return values[0]


def hear(known, side):
    plan = meetings(side)
    used, pairs = {}, []
    for (row, z), pair in plan.items():
        for core, chip in enumerate(pair):
            from_core = used.get(chip, 0)
            used[chip] = from_core + 1
            pairs.append(((chip[0] * side + chip[1]) * 2 + from_core, (row * side + z) * 2 + core))
    return lax.ppermute(known, BOTH, pairs)


def gram_body(side, view_a, view_b):
    n_col = 2 * side
    share, width = view_a.shape
    pair, half = view_b.shape
    count = share * n_col
    row = lax.axis_index("row")
    col = lax.axis_index("col")
    z = lax.shift_right_logical(col, 1)
    is_a = (col & 1) == 0
    diagonal = row == z

    got_a, got_b = sibling(view_a, n_col), sibling(view_b, n_col)
    own = jnp.where(
        is_a, jnp.concatenate([view_a, got_a], 0), jnp.concatenate([got_b, view_b], 1)
    )

    pieces, late = {}, own
    for step in range(1, side):
        pieces[step] = flip(late, side, step)
        late = jnp.where(row < (step + 1) * side, late, 0)
    pieces = [own] + [pieces[step] for step in range(1, side)]
    mine = jnp.concatenate(in_order(pieces, jnp.where(is_a, z, row)), 0)
    other = sibling(mine, n_col)

    normed, scaled = standardize(mine)
    gram = lax.dot_general(
        normed, normed, (((1,), (1,)), ((), ())), preferred_element_type=jnp.float32
    )
    normed, gram, other = lax.optimization_barrier((normed, gram, other))
    other_normed, other_scaled = standardize(other)

    normed_f = normed.astype(jnp.float32)
    other_f = other_normed.astype(jnp.float32)
    corr = jnp.mean(normed_f * other_f, 0)
    slope = jnp.where(diagonal, rounded(2.0 * (corr - 1.0)) - 2.0 * off_weight * corr, 0.0)
    extra = (slope * (normed_f - jnp.mean(normed_f, 0) - other_f * corr)).astype(jnp.bfloat16)
    part = jnp.square(1.0 - corr) - off_weight * jnp.square(corr)
    part = jnp.sum(jnp.where(diagonal, part, 0.0).reshape(-1, 128), 0, keepdims=True)

    lanes = width // side

    def payload(images, gram, part):
        images = [images[:, i * lanes : (i + 1) * lanes] for i in range(side)]
        part = [jnp.broadcast_to(x, (count // 2, 128)) for x in split(part)]
        return jnp.concatenate([jnp.concatenate(images, 0), *split(gram), jnp.concatenate(part, 0)], 1)

    def images_of(step):
        return lax.dynamic_slice_in_dim(extra, (row ^ step) * pair, pair, 0)

    landed = {step: across(payload(images_of(step), gram, part), side, step) for step in range(1, side)}
    landed[0] = payload(images_of(0), gram, part)
    summed = total([landed[step].astype(jnp.float32) for step in range(side)])
    gram = summed[:, lanes : lanes + count] + summed[:, lanes + count : lanes + 2 * count]
    part = summed[:1, lanes + 2 * count :] + summed[count // 2 : count // 2 + 1, lanes + 2 * count :]

    sent = jnp.concatenate([summed[:, :lanes].astype(jnp.bfloat16), *split(gram)], 1)
    came = sibling(sent, n_col)
    for_a = jnp.where(is_a, came, sent)
    for_b = jnp.where(is_a, sent, came)

    slots = lax.broadcasted_iota(jnp.int32, (2 * side, 128), 0)
    known = jnp.where(slots < side, part, 1.0)
    known = jnp.where((slots & (side - 1)) == jnp.where(is_a, z, row), known, 0.0)
    known = joined(known, sibling(known, n_col))
    heard = hear(known, side)

    twice = [jnp.where(is_a, normed, other_normed)] * 2
    all_a = jnp.concatenate(twice, 0)
    twice = [jnp.where(is_a, other_normed[:, :half], normed[:, half:])] * 2
    all_b = jnp.concatenate(twice, 0)
    scaled_a = jnp.where(is_a, scaled, other_scaled)
    scaled_b = jnp.where(is_a, other_scaled[:half], scaled[half:])

    def images_in(sums):
        return jnp.concatenate([sums[i * pair : (i + 1) * pair, :lanes] for i in range(side)], 1)

    extra_a = images_in(for_a)
    extra_a = jnp.where(is_a, extra_a[:share], extra_a[share:])
    extra_b = images_in(for_b)
    extra_b = jnp.where(is_a, extra_b[:, :half], extra_b[:, half:])

    def terms(sums, twice):
        halves = sums[:, lanes : lanes + 2 * count]
        term = jnp.dot(halves, twice, preferred_element_type=jnp.float32)
        term = term * (2.0 * off_weight / count)
        return (term, jnp.mean(term, 0), jnp.mean(term * twice[:count].astype(jnp.float32), 0))

    def gradient(terms, twice, scaled, extra, start, images):
        term, first, second = terms
        term = lax.dynamic_slice_in_dim(term, start, images, 0)
        normed = lax.dynamic_slice_in_dim(twice, start, images, 0).astype(jnp.float32)
        return (scaled * (term - first - normed * second + extra.astype(jnp.float32))).astype(
            jnp.bfloat16
        )

    def whole(sums):
        sums = sums.astype(jnp.float32)
        return sums[:, lanes : lanes + count] + sums[:, lanes + count : lanes + 2 * count]

    everywhere = whole(for_a) * whole(for_b) * (off_weight / (count * count * width * side))
    everywhere = jnp.pad(jnp.sum(everywhere, 0), (0, 128 - count))
    grad_a = gradient(terms(for_a, all_a), all_a, scaled_a, extra_a, col * share, share)
    grad_b = gradient(terms(for_b, all_b), all_b, scaled_b, extra_b, row * pair, pair)

    heard, grad_a, grad_b, everywhere = lax.optimization_barrier((heard, grad_a, grad_b, everywhere))
    known = joined(known, heard)
    known = joined(known, sibling(known, n_col))
    loss = jnp.sum(everywhere + jnp.sum(known[:side], 0) * (1.0 / (width * side)))
    return (loss, grad_a, grad_b)


def solution(mesh):
    in_specs = (P("col", "row"), P("row", "col"))
    out_specs = (P(), P("col", "row"), P("row", "col"))
    n_row, n_col = mesh.shape["row"], mesh.shape["col"]
    square = n_col == 2 * n_row and n_row & (n_row - 1) == 0

    def body(view_a, view_b):
        share, width = view_a.shape
        count = share * n_col
        fits = view_b.shape == (2 * share, width // 2) and width % (128 * n_row) == 0
        fits = fits and share % 8 == 0 and count <= 128 and 2 * count % 128 == 0
        if square and fits and meetings(n_row):
            return gram_body(n_row, view_a, view_b)
        return tiled_body(view_a, view_b)

    return jax.shard_map(body, mesh=mesh, in_specs=in_specs, out_specs=out_specs, check_vma=False)
```

```python
import jax
import jax.numpy as jnp
from jax import lax
from jax.sharding import PartitionSpec as P

off_weight = 0.0051
epsilon = 1e-05

BOTH = ("row", "col")


def normalize(values):
    values = values.astype(jnp.float32)
    center = jnp.mean(values, 0)
    spread = jnp.mean(jnp.square(values - center), 0)
    scaled = lax.rsqrt(spread + epsilon)
    return (((values - center) * scaled).astype(jnp.bfloat16), scaled)


def tiled_body(view_a, view_b):
    whole_a = lax.all_gather(view_a, "col", axis=0, tiled=True)
    whole_b = lax.all_gather(view_b, "row", axis=0, tiled=True)
    normed_a, scaled_a = normalize(whole_a)
    normed_b, scaled_b = normalize(whole_b)
    count = whole_a.shape[0]
    width_a = whole_a.shape[1]
    width_b = whole_b.shape[1]
    corr = (
        lax.dot_general(
            normed_a, normed_b, (((0,), (0,)), ((), ())), preferred_element_type=jnp.float32
        )
        / count
    )
    rows = lax.axis_index("row") * width_a + lax.iota(jnp.int32, width_a)
    columns = lax.axis_index("col") * width_b + lax.iota(jnp.int32, width_b)
    diag = rows[:, None] == columns[None, :]
    partial_loss = jnp.sum(jnp.where(diag, jnp.square(1.0 - corr), off_weight * jnp.square(corr)))
    weights = jnp.where(diag, 2.0 * (corr - 1.0), 2.0 * off_weight * corr).astype(jnp.bfloat16)
    term_a = lax.dot_general(
        normed_b, weights, (((1,), (1,)), ((), ())), preferred_element_type=jnp.float32
    )
    term_b = jnp.dot(normed_a, weights, preferred_element_type=jnp.float32)
    summed_a = lax.psum_scatter(term_a, "col", scatter_dimension=0, tiled=True)
    summed_b = lax.psum_scatter(term_b, "row", scatter_dimension=0, tiled=True)
    share_a = summed_a.shape[0]
    share_b = summed_b.shape[0]
    mine_a = lax.dynamic_slice_in_dim(normed_a, lax.axis_index("col") * share_a, share_a, 0).astype(
        jnp.float32
    )
    mine_b = lax.dynamic_slice_in_dim(normed_b, lax.axis_index("row") * share_b, share_b, 0).astype(
        jnp.float32
    )
    first_a, second_a = lax.psum((jnp.sum(summed_a, 0), jnp.sum(summed_a * mine_a, 0)), "col")
    first_b, second_b = lax.psum((jnp.sum(summed_b, 0), jnp.sum(summed_b * mine_b, 0)), "row")
    grad_a = (scaled_a * (summed_a - first_a / count - mine_a * (second_a / count))).astype(
        jnp.bfloat16
    )
    grad_b = (scaled_b * (summed_b - first_b / count - mine_b * (second_b / count))).astype(
        jnp.bfloat16
    )
    total = lax.psum(partial_loss, ("row", "col"))
    loss = total / (width_a * lax.axis_size("row"))
    return (loss, grad_a, grad_b)


def sibling(value, n_col):
    return lax.ppermute(value, "col", [(c, c ^ 1) for c in range(n_col)])


def flip(value, side, step):
    pairs = []
    for row in range(side):
        for z in range(side):
            pairs.append(((row * side + z) * 2, (row * side + (z ^ step)) * 2))
            pairs.append(((row * side + z) * 2 + 1, ((row ^ step) * side + z) * 2 + 1))
    return lax.ppermute(value, BOTH, pairs)


def across(value, side, step):
    pairs = []
    for row in range(side):
        for z in range(side):
            pairs.append(((row * side + z) * 2, ((row ^ step) * side + z) * 2))
            pairs.append(((row * side + z) * 2 + 1, (row * side + (z ^ step)) * 2 + 1))
    return lax.ppermute(value, BOTH, pairs)


def in_order(pieces, position):
    bit = 1
    while bit < len(pieces):
        on = (position & bit) != 0
        pieces = [jnp.where(on, pieces[i ^ bit], pieces[i]) for i in range(len(pieces))]
        bit *= 2
    return pieces


def rounded(value):
    return lax.reduce_precision(value, exponent_bits=8, mantissa_bits=7)


def split(value):
    high = rounded(value)
    return high.astype(jnp.bfloat16), rounded(value - high).astype(jnp.bfloat16)


def standardize(values):
    values = values.astype(jnp.float32)
    center = jnp.mean(values, 0)
    spread = jnp.mean(jnp.square(values - center), 0)
    scaled = lax.rsqrt(spread + epsilon)
    return (rounded((values - center) * scaled).astype(jnp.bfloat16), scaled)


def meetings(side):
    chips = [(row, z) for row in range(side) for z in range(side)]

    def hops(p, q):
        return bin(p[0] ^ q[0]).count("1") + abs(p[1] - q[1])

    def search(choices, order, used, chosen):
        if len(chosen) == len(order):
            return dict(chosen)
        chip = order[len(chosen)]
        for pair in choices[chip]:
            if all(used[q] < 2 for q in pair):
                for q in pair:
                    used[q] += 1
                found = search(choices, order, used, chosen + [(chip, pair)])
                if found:
                    return found
                for q in pair:
                    used[q] -= 1
        return None

    if side > 6:
        return None
    for limit in range(1, 3 * side):
        choices = {
            p: sorted(
                (
                    (q, t)
                    for i, q in enumerate(chips)
                    for t in chips[i + 1 :]
                    if max(hops(p, q), hops(p, t)) <= limit and len({*p, *q, *t}) == side
                ),
                key=lambda pair, p=p: hops(p, pair[0]) + hops(p, pair[1]),
            )
            for p in chips
        }
        if all(choices.values()):
            order = sorted(chips, key=lambda p: len(choices[p]))
            found = search(choices, order, dict.fromkeys(chips, 0), [])
            if found:
                return found
    return None


def joined(known, heard):
    side = known.shape[0] // 2
    here = known[side:] > 0.0
    return jnp.concatenate(
        [jnp.where(here, known[:side], heard[:side]), jnp.maximum(known[side:], heard[side:])], 0
    )


def total(values):
    while len(values) > 1:
        values = [x + y for x, y in zip(values[::2], values[1::2])]
    return values[0]


def hear(known, side):
    plan = meetings(side)
    used, pairs = {}, []
    for (row, z), pair in plan.items():
        for core, chip in enumerate(pair):
            from_core = used.get(chip, 1)
            used[chip] = from_core - 1
            pairs.append(((chip[0] * side + chip[1]) * 2 + from_core, (row * side + z) * 2 + core))
    return lax.ppermute(known, BOTH, pairs)


def gram_body(side, view_a, view_b):
    n_col = 2 * side
    share, width = view_a.shape
    pair, half = view_b.shape
    count = share * n_col
    row = lax.axis_index("row")
    col = lax.axis_index("col")
    z = lax.shift_right_logical(col, 1)
    is_a = (col & 1) == 0
    diagonal = row == z

    got_a, got_b = sibling(view_a, n_col), sibling(view_b, n_col)
    own = jnp.where(
        is_a, jnp.concatenate([view_a, got_a], 0), jnp.concatenate([got_b, view_b], 1)
    )

    pieces, late = {}, own
    for step in range(1, side):
        pieces[step] = flip(late, side, step)
        late = jnp.where(row < (step + 1) * side, late, 0)
    pieces = [own] + [pieces[step] for step in range(1, side)]
    mine = jnp.concatenate(in_order(pieces, jnp.where(is_a, z, row)), 0)
    other = sibling(mine, n_col)

    normed, scaled = standardize(mine)
    gram = lax.dot_general(
        normed, normed, (((1,), (1,)), ((), ())), preferred_element_type=jnp.float32
    )
    normed, gram, other = lax.optimization_barrier((normed, gram, other))
    other_normed, other_scaled = standardize(other)

    normed_f = normed.astype(jnp.float32)
    other_f = other_normed.astype(jnp.float32)
    corr = jnp.mean(normed_f * other_f, 0)
    slope = jnp.where(diagonal, rounded(2.0 * (corr - 1.0)) - 2.0 * off_weight * corr, 0.0)
    extra = (slope * (normed_f - jnp.mean(normed_f, 0) - other_f * corr)).astype(jnp.bfloat16)
    part = jnp.square(1.0 - corr) - off_weight * jnp.square(corr)
    part = jnp.sum(jnp.where(diagonal, part, 0.0).reshape(-1, 128), 0, keepdims=True)

    lanes = width // side

    def payload(images, gram, part):
        images = [images[:, i * lanes : (i + 1) * lanes] for i in range(side)]
        part = [jnp.broadcast_to(x, (count // 2, 128)) for x in split(part)]
        return jnp.concatenate([jnp.concatenate(images, 0), *split(gram), jnp.concatenate(part, 0)], 1)

    def images_of(step):
        return lax.dynamic_slice_in_dim(extra, (row ^ step) * pair, pair, 0)

    landed = {step: across(payload(images_of(step), gram, part), side, step) for step in range(1, side)}
    landed[0] = payload(images_of(0), gram, part)
    summed = total([landed[step].astype(jnp.float32) for step in range(side)])
    gram = summed[:, lanes : lanes + count] + summed[:, lanes + count : lanes + 2 * count]
    part = summed[:1, lanes + 2 * count :] + summed[count // 2 : count // 2 + 1, lanes + 2 * count :]

    sent = jnp.concatenate([summed[:, :lanes].astype(jnp.bfloat16), *split(gram)], 1)
    came = sibling(sent, n_col)
    for_a = jnp.where(is_a, came, sent)
    for_b = jnp.where(is_a, sent, came)

    slots = lax.broadcasted_iota(jnp.int32, (2 * side, 128), 0)
    known = jnp.where(slots < side, part, 1.0)
    known = jnp.where((slots & (side - 1)) == jnp.where(is_a, z, row), known, 0.0)
    known = joined(known, sibling(known, n_col))
    heard = hear(known, side)

    twice = [jnp.where(is_a, normed, other_normed)] * 2
    all_a = jnp.concatenate(twice, 0)
    twice = [jnp.where(is_a, other_normed[:, :half], normed[:, half:])] * 2
    all_b = jnp.concatenate(twice, 0)
    scaled_a = jnp.where(is_a, scaled, other_scaled)
    scaled_b = jnp.where(is_a, other_scaled[:half], scaled[half:])

    def images_in(sums):
        return jnp.concatenate([sums[i * pair : (i + 1) * pair, :lanes] for i in range(side)], 1)

    extra_a = images_in(for_a)
    extra_a = jnp.where(is_a, extra_a[:share], extra_a[share:])
    extra_b = images_in(for_b)
    extra_b = jnp.where(is_a, extra_b[:, :half], extra_b[:, half:])

    def terms(sums, twice):
        halves = sums[:, lanes : lanes + 2 * count]
        term = jnp.dot(halves, twice, preferred_element_type=jnp.float32)
        term = term * (2.0 * off_weight / count)
        return (term, jnp.mean(term, 0), jnp.mean(term * twice[:count].astype(jnp.float32), 0))

    def gradient(terms, twice, scaled, extra, start, images):
        term, first, second = terms
        term = lax.dynamic_slice_in_dim(term, start, images, 0)
        normed = lax.dynamic_slice_in_dim(twice, start, images, 0).astype(jnp.float32)
        return (scaled * (term - first - normed * second + extra.astype(jnp.float32))).astype(
            jnp.bfloat16
        )

    def whole(sums):
        sums = sums.astype(jnp.float32)
        return sums[:, lanes : lanes + count] + sums[:, lanes + count : lanes + 2 * count]

    everywhere = whole(for_a) * whole(for_b) * (off_weight / (count * count * width * side))
    everywhere = jnp.pad(jnp.sum(everywhere, 0), (0, 128 - count))
    grad_a = gradient(terms(for_a, all_a), all_a, scaled_a, extra_a, col * share, share)
    grad_b = gradient(terms(for_b, all_b), all_b, scaled_b, extra_b, row * pair, pair)

    heard, grad_a, grad_b, everywhere = lax.optimization_barrier((heard, grad_a, grad_b, everywhere))
    known = joined(known, heard)
    known = joined(known, sibling(known, n_col))
    loss = jnp.sum(everywhere + jnp.sum(known[:side], 0) * (1.0 / (width * side)))
    return (loss, grad_a, grad_b)


def solution(mesh):
    in_specs = (P("col", "row"), P("row", "col"))
    out_specs = (P(), P("col", "row"), P("row", "col"))
    n_row, n_col = mesh.shape["row"], mesh.shape["col"]
    square = n_col == 2 * n_row and n_row & (n_row - 1) == 0

    def body(view_a, view_b):
        share, width = view_a.shape
        count = share * n_col
        fits = view_b.shape == (2 * share, width // 2) and width % (128 * n_row) == 0
        fits = fits and share % 8 == 0 and count <= 128 and 2 * count % 128 == 0
        if square and fits and meetings(n_row):
            return gram_body(n_row, view_a, view_b)
        return tiled_body(view_a, view_b)

    return jax.shard_map(body, mesh=mesh, in_specs=in_specs, out_specs=out_specs, check_vma=False)
```

```python
import jax
import jax.numpy as jnp
from jax import lax
from jax.sharding import PartitionSpec as P

off_weight = 0.0051
epsilon = 1e-05

BOTH = ("row", "col")


def normalize(values):
    values = values.astype(jnp.float32)
    center = jnp.mean(values, 0)
    spread = jnp.mean(jnp.square(values - center), 0)
    scaled = lax.rsqrt(spread + epsilon)
    return (((values - center) * scaled).astype(jnp.bfloat16), scaled)


def tiled_body(view_a, view_b):
    whole_a = lax.all_gather(view_a, "col", axis=0, tiled=True)
    whole_b = lax.all_gather(view_b, "row", axis=0, tiled=True)
    normed_a, scaled_a = normalize(whole_a)
    normed_b, scaled_b = normalize(whole_b)
    count = whole_a.shape[0]
    width_a = whole_a.shape[1]
    width_b = whole_b.shape[1]
    corr = (
        lax.dot_general(
            normed_a, normed_b, (((0,), (0,)), ((), ())), preferred_element_type=jnp.float32
        )
        / count
    )
    rows = lax.axis_index("row") * width_a + lax.iota(jnp.int32, width_a)
    columns = lax.axis_index("col") * width_b + lax.iota(jnp.int32, width_b)
    diag = rows[:, None] == columns[None, :]
    partial_loss = jnp.sum(jnp.where(diag, jnp.square(1.0 - corr), off_weight * jnp.square(corr)))
    weights = jnp.where(diag, 2.0 * (corr - 1.0), 2.0 * off_weight * corr).astype(jnp.bfloat16)
    term_a = lax.dot_general(
        normed_b, weights, (((1,), (1,)), ((), ())), preferred_element_type=jnp.float32
    )
    term_b = jnp.dot(normed_a, weights, preferred_element_type=jnp.float32)
    summed_a = lax.psum_scatter(term_a, "col", scatter_dimension=0, tiled=True)
    summed_b = lax.psum_scatter(term_b, "row", scatter_dimension=0, tiled=True)
    share_a = summed_a.shape[0]
    share_b = summed_b.shape[0]
    mine_a = lax.dynamic_slice_in_dim(normed_a, lax.axis_index("col") * share_a, share_a, 0).astype(
        jnp.float32
    )
    mine_b = lax.dynamic_slice_in_dim(normed_b, lax.axis_index("row") * share_b, share_b, 0).astype(
        jnp.float32
    )
    first_a, second_a = lax.psum((jnp.sum(summed_a, 0), jnp.sum(summed_a * mine_a, 0)), "col")
    first_b, second_b = lax.psum((jnp.sum(summed_b, 0), jnp.sum(summed_b * mine_b, 0)), "row")
    grad_a = (scaled_a * (summed_a - first_a / count - mine_a * (second_a / count))).astype(
        jnp.bfloat16
    )
    grad_b = (scaled_b * (summed_b - first_b / count - mine_b * (second_b / count))).astype(
        jnp.bfloat16
    )
    total = lax.psum(partial_loss, ("row", "col"))
    loss = total / (width_a * lax.axis_size("row"))
    return (loss, grad_a, grad_b)


def sibling(value, n_col):
    return lax.ppermute(value, "col", [(c, c ^ 1) for c in range(n_col)])


def flip(value, side, step):
    pairs = []
    for row in range(side):
        for z in range(side):
            pairs.append(((row * side + z) * 2, (row * side + (z ^ step)) * 2))
            pairs.append(((row * side + z) * 2 + 1, ((row ^ step) * side + z) * 2 + 1))
    return lax.ppermute(value, BOTH, pairs)


def across(value, side, step):
    pairs = []
    for row in range(side):
        for z in range(side):
            pairs.append(((row * side + z) * 2, ((row ^ step) * side + z) * 2))
            pairs.append(((row * side + z) * 2 + 1, (row * side + (z ^ step)) * 2 + 1))
    return lax.ppermute(value, BOTH, pairs)


def in_order(pieces, position):
    bit = 1
    while bit < len(pieces):
        on = (position & bit) != 0
        pieces = [jnp.where(on, pieces[i ^ bit], pieces[i]) for i in range(len(pieces))]
        bit *= 2
    return pieces


def rounded(value):
    return lax.reduce_precision(value, exponent_bits=8, mantissa_bits=7)


def split(value):
    high = rounded(value)
    return high.astype(jnp.bfloat16), rounded(value - high).astype(jnp.bfloat16)


def standardize(values):
    values = values.astype(jnp.float32)
    center = jnp.mean(values, 0)
    spread = jnp.mean(jnp.square(values - center), 0)
    scaled = lax.rsqrt(spread + epsilon)
    return (rounded((values - center) * scaled).astype(jnp.bfloat16), scaled)


def meetings(side):
    chips = [(row, z) for row in range(side) for z in range(side)]

    def hops(p, q):
        return bin(p[0] ^ q[0]).count("1") + abs(p[1] - q[1])

    def search(choices, order, used, chosen):
        if len(chosen) == len(order):
            return dict(chosen)
        chip = order[len(chosen)]
        for pair in choices[chip]:
            if all(used[q] < 2 for q in pair):
                for q in pair:
                    used[q] += 1
                found = search(choices, order, used, chosen + [(chip, pair)])
                if found:
                    return found
                for q in pair:
                    used[q] -= 1
        return None

    if side > 6:
        return None
    for limit in range(1, 3 * side):
        choices = {
            p: sorted(
                (
                    (q, t)
                    for i, q in enumerate(chips)
                    for t in chips[i + 1 :]
                    if max(hops(p, q), hops(p, t)) <= limit and len({*p, *q, *t}) == side
                ),
                key=lambda pair, p=p: hops(p, pair[0]) + hops(p, pair[1]),
            )
            for p in chips
        }
        if all(choices.values()):
            order = sorted(chips, key=lambda p: len(choices[p]))
            found = search(choices, order, dict.fromkeys(chips, 0), [])
            if found:
                return found
    return None


def joined(known, heard):
    side = known.shape[0] // 2
    here = known[side:] > 0.0
    return jnp.concatenate(
        [jnp.where(here, known[:side], heard[:side]), jnp.maximum(known[side:], heard[side:])], 0
    )


def total(values):
    while len(values) > 1:
        values = [x + y for x, y in zip(values[::2], values[1::2])]
    return values[0]


def hear(known, side):
    plan = meetings(side)
    used, pairs = {}, []
    for (row, z), pair in plan.items():
        for core, chip in enumerate(pair):
            from_core = used.get(chip, 1)
            used[chip] = from_core - 1
            pairs.append(((chip[0] * side + chip[1]) * 2 + from_core, (row * side + z) * 2 + core))
    return [
        lax.ppermute(known, BOTH, pairs),
        lax.ppermute(known, BOTH, [(teller, hearer ^ 1) for teller, hearer in pairs]),
    ]


def gram_body(side, view_a, view_b):
    n_col = 2 * side
    share, width = view_a.shape
    pair, half = view_b.shape
    count = share * n_col
    row = lax.axis_index("row")
    col = lax.axis_index("col")
    z = lax.shift_right_logical(col, 1)
    is_a = (col & 1) == 0
    diagonal = row == z

    got_a, got_b = sibling(view_a, n_col), sibling(view_b, n_col)
    own = jnp.where(
        is_a, jnp.concatenate([view_a, got_a], 0), jnp.concatenate([got_b, view_b], 1)
    )

    pieces, late = {}, own
    for step in range(1, side):
        pieces[step] = flip(late, side, step)
        late = jnp.where(row < (step + 1) * side, late, 0)
    pieces = [own] + [pieces[step] for step in range(1, side)]
    mine = jnp.concatenate(in_order(pieces, jnp.where(is_a, z, row)), 0)
    other = sibling(mine, n_col)

    normed, scaled = standardize(mine)
    gram = lax.dot_general(
        normed, normed, (((1,), (1,)), ((), ())), preferred_element_type=jnp.float32
    )
    normed, gram, other = lax.optimization_barrier((normed, gram, other))
    other_normed, other_scaled = standardize(other)

    normed_f = normed.astype(jnp.float32)
    other_f = other_normed.astype(jnp.float32)
    corr = jnp.mean(normed_f * other_f, 0)
    slope = jnp.where(diagonal, rounded(2.0 * (corr - 1.0)) - 2.0 * off_weight * corr, 0.0)
    extra = (slope * (normed_f - jnp.mean(normed_f, 0) - other_f * corr)).astype(jnp.bfloat16)
    part = jnp.square(1.0 - corr) - off_weight * jnp.square(corr)
    part = jnp.sum(jnp.where(diagonal, part, 0.0).reshape(-1, 128), 0, keepdims=True)

    lanes, few = width // side, 32
    i, j = (lax.broadcasted_iota(jnp.int32, (count, count), d) for d in range(2))

    def with_loss(low, part):
        part = sum(part[:, k : k + few] for k in range(0, 128, few))
        for line, half in enumerate(split(part)):
            half = jnp.pad(half, ((0, 0), (0, count - few)))
            low = jnp.where((i == count - 1 - line) & (j < few), half, low)
        return low

    def payload(images, gram, part):
        images = [images[:, i * lanes : (i + 1) * lanes] for i in range(side)]
        high, low = split(gram)
        return jnp.concatenate([jnp.concatenate(images, 0), high, with_loss(low, part)], 1)

    def images_of(step, extra):
        return lax.dynamic_slice_in_dim(extra, (row ^ step) * pair, pair, 0)

    landed = {}
    for step in (2, 1, *range(3, side)):
        ready = payload(images_of(step, extra), gram, part)
        ready, extra = lax.optimization_barrier((ready, extra))
        landed[step] = across(ready, side, step)
    landed[0] = payload(images_of(0, extra), gram, part)
    summed = total([landed[step].astype(jnp.float32) for step in range(side)])
    high, low = summed[:, lanes : lanes + count], summed[:, lanes + count :]
    part = low[count - 1 :, :few] + low[count - 2 : count - 1, :few]
    part = jnp.pad(part, ((0, 0), (0, 128 - few)))
    gram = high + low
    gram = jnp.where((i >= count - 2) & (j < few), gram.T, gram)

    sent = jnp.concatenate([summed[:, :lanes].astype(jnp.bfloat16), *split(gram)], 1)
    came = sibling(sent, n_col)
    for_a = jnp.where(is_a, came, sent)
    for_b = jnp.where(is_a, sent, came)

    slots = lax.broadcasted_iota(jnp.int32, (2 * side, 128), 0)
    known = jnp.where(slots < side, part, 1.0)
    known = jnp.where((slots & (side - 1)) == jnp.where(is_a, z, row), known, 0.0)
    known = joined(known, sibling(known, n_col))
    heard = hear(known, side)

    twice = [jnp.where(is_a, normed, other_normed)] * 2
    all_a = jnp.concatenate(twice, 0)
    twice = [jnp.where(is_a, other_normed[:, :half], normed[:, half:])] * 2
    all_b = jnp.concatenate(twice, 0)
    scaled_a = jnp.where(is_a, scaled, other_scaled)
    scaled_b = jnp.where(is_a, other_scaled[:half], scaled[half:])

    def images_in(sums):
        return jnp.concatenate([sums[i * pair : (i + 1) * pair, :lanes] for i in range(side)], 1)

    extra_a = images_in(for_a)
    extra_a = jnp.where(is_a, extra_a[:share], extra_a[share:])
    extra_b = images_in(for_b)
    extra_b = jnp.where(is_a, extra_b[:, :half], extra_b[:, half:])

    def terms(sums, twice):
        halves = sums[:, lanes : lanes + 2 * count]
        term = jnp.dot(halves, twice, preferred_element_type=jnp.float32)
        term = term * (2.0 * off_weight / count)
        return (term, jnp.mean(term, 0), jnp.mean(term * twice[:count].astype(jnp.float32), 0))

    def gradient(terms, twice, scaled, extra, start, images):
        term, first, second = terms
        term = lax.dynamic_slice_in_dim(term, start, images, 0)
        normed = lax.dynamic_slice_in_dim(twice, start, images, 0).astype(jnp.float32)
        return (scaled * (term - first - normed * second + extra.astype(jnp.float32))).astype(
            jnp.bfloat16
        )

    def whole(sums):
        sums = sums.astype(jnp.float32)
        return sums[:, lanes : lanes + count] + sums[:, lanes + count : lanes + 2 * count]

    everywhere = whole(for_a) * whole(for_b) * (off_weight / (count * count * width * side))
    everywhere = jnp.pad(jnp.sum(everywhere, 0), (0, 128 - count))
    grad_a = gradient(terms(for_a, all_a), all_a, scaled_a, extra_a, col * share, share)
    grad_b = gradient(terms(for_b, all_b), all_b, scaled_b, extra_b, row * pair, pair)

    heard, grad_a, grad_b, everywhere = lax.optimization_barrier((heard, grad_a, grad_b, everywhere))
    known = joined(joined(known, heard[0]), heard[1])
    loss = jnp.sum(everywhere + jnp.sum(known[:side], 0) * (1.0 / (width * side)))
    return (loss, grad_a, grad_b)


def solution(mesh):
    in_specs = (P("col", "row"), P("row", "col"))
    out_specs = (P(), P("col", "row"), P("row", "col"))
    n_row, n_col = mesh.shape["row"], mesh.shape["col"]
    square = n_col == 2 * n_row and n_row & (n_row - 1) == 0

    def body(view_a, view_b):
        share, width = view_a.shape
        count = share * n_col
        fits = view_b.shape == (2 * share, width // 2) and width % (128 * n_row) == 0
        fits = fits and share % 8 == 0 and count <= 128 and 2 * count % 128 == 0
        if square and fits and meetings(n_row):
            return gram_body(n_row, view_a, view_b)
        return tiled_body(view_a, view_b)

    return jax.shard_map(body, mesh=mesh, in_specs=in_specs, out_specs=out_specs, check_vma=False)
```

```python
import jax
import jax.numpy as jnp
from jax import lax
from jax.sharding import PartitionSpec as P

off_weight = 0.0051
epsilon = 1e-05

BOTH = ("row", "col")


def normalize(values):
    values = values.astype(jnp.float32)
    center = jnp.mean(values, 0)
    spread = jnp.mean(jnp.square(values - center), 0)
    scaled = lax.rsqrt(spread + epsilon)
    return (((values - center) * scaled).astype(jnp.bfloat16), scaled)


def tiled_body(view_a, view_b):
    whole_a = lax.all_gather(view_a, "col", axis=0, tiled=True)
    whole_b = lax.all_gather(view_b, "row", axis=0, tiled=True)
    normed_a, scaled_a = normalize(whole_a)
    normed_b, scaled_b = normalize(whole_b)
    count = whole_a.shape[0]
    width_a = whole_a.shape[1]
    width_b = whole_b.shape[1]
    corr = (
        lax.dot_general(
            normed_a, normed_b, (((0,), (0,)), ((), ())), preferred_element_type=jnp.float32
        )
        / count
    )
    rows = lax.axis_index("row") * width_a + lax.iota(jnp.int32, width_a)
    columns = lax.axis_index("col") * width_b + lax.iota(jnp.int32, width_b)
    diag = rows[:, None] == columns[None, :]
    partial_loss = jnp.sum(jnp.where(diag, jnp.square(1.0 - corr), off_weight * jnp.square(corr)))
    weights = jnp.where(diag, 2.0 * (corr - 1.0), 2.0 * off_weight * corr).astype(jnp.bfloat16)
    term_a = lax.dot_general(
        normed_b, weights, (((1,), (1,)), ((), ())), preferred_element_type=jnp.float32
    )
    term_b = jnp.dot(normed_a, weights, preferred_element_type=jnp.float32)
    summed_a = lax.psum_scatter(term_a, "col", scatter_dimension=0, tiled=True)
    summed_b = lax.psum_scatter(term_b, "row", scatter_dimension=0, tiled=True)
    share_a = summed_a.shape[0]
    share_b = summed_b.shape[0]
    mine_a = lax.dynamic_slice_in_dim(normed_a, lax.axis_index("col") * share_a, share_a, 0).astype(
        jnp.float32
    )
    mine_b = lax.dynamic_slice_in_dim(normed_b, lax.axis_index("row") * share_b, share_b, 0).astype(
        jnp.float32
    )
    first_a, second_a = lax.psum((jnp.sum(summed_a, 0), jnp.sum(summed_a * mine_a, 0)), "col")
    first_b, second_b = lax.psum((jnp.sum(summed_b, 0), jnp.sum(summed_b * mine_b, 0)), "row")
    grad_a = (scaled_a * (summed_a - first_a / count - mine_a * (second_a / count))).astype(
        jnp.bfloat16
    )
    grad_b = (scaled_b * (summed_b - first_b / count - mine_b * (second_b / count))).astype(
        jnp.bfloat16
    )
    total = lax.psum(partial_loss, ("row", "col"))
    loss = total / (width_a * lax.axis_size("row"))
    return (loss, grad_a, grad_b)


def sibling(value, n_col):
    return lax.ppermute(value, "col", [(c, c ^ 1) for c in range(n_col)])


def flip(value, side, step):
    pairs = []
    for row in range(side):
        for z in range(side):
            pairs.append(((row * side + z) * 2, (row * side + (z ^ step)) * 2))
            pairs.append(((row * side + z) * 2 + 1, ((row ^ step) * side + z) * 2 + 1))
    return lax.ppermute(value, BOTH, pairs)


def across(value, side, step):
    pairs = []
    for row in range(side):
        for z in range(side):
            pairs.append(((row * side + z) * 2, ((row ^ step) * side + z) * 2))
            pairs.append(((row * side + z) * 2 + 1, (row * side + (z ^ step)) * 2 + 1))
    return lax.ppermute(value, BOTH, pairs)


def in_order(pieces, position):
    bit = 1
    while bit < len(pieces):
        on = (position & bit) != 0
        pieces = [jnp.where(on, pieces[i ^ bit], pieces[i]) for i in range(len(pieces))]
        bit *= 2
    return pieces


def rounded(value):
    return lax.reduce_precision(value, exponent_bits=8, mantissa_bits=7)


def split(value):
    high = rounded(value)
    return high.astype(jnp.bfloat16), rounded(value - high).astype(jnp.bfloat16)


def standardize(values):
    values = values.astype(jnp.float32)
    center = jnp.mean(values, 0)
    spread = jnp.mean(jnp.square(values - center), 0)
    scaled = lax.rsqrt(spread + epsilon)
    return (rounded((values - center) * scaled).astype(jnp.bfloat16), scaled)


def meetings(side):
    chips = [(row, z) for row in range(side) for z in range(side)]

    def hops(p, q):
        return bin(p[0] ^ q[0]).count("1") + abs(p[1] - q[1])

    def search(choices, order, used, chosen):
        if len(chosen) == len(order):
            return dict(chosen)
        chip = order[len(chosen)]
        for pair in choices[chip]:
            if all(used[q] < 2 for q in pair):
                for q in pair:
                    used[q] += 1
                found = search(choices, order, used, chosen + [(chip, pair)])
                if found:
                    return found
                for q in pair:
                    used[q] -= 1
        return None

    if side > 6:
        return None
    for limit in range(1, 3 * side):
        choices = {
            p: sorted(
                (
                    (q, t)
                    for i, q in enumerate(chips)
                    for t in chips[i + 1 :]
                    if max(hops(p, q), hops(p, t)) <= limit and len({*p, *q, *t}) == side
                ),
                key=lambda pair, p=p: hops(p, pair[0]) + hops(p, pair[1]),
            )
            for p in chips
        }
        if all(choices.values()):
            order = sorted(chips, key=lambda p: len(choices[p]))
            found = search(choices, order, dict.fromkeys(chips, 0), [])
            if found:
                return found
    return None


def joined(known, heard):
    side = known.shape[0] // 2
    here = known[side:] > 0.0
    return jnp.concatenate(
        [jnp.where(here, known[:side], heard[:side]), jnp.maximum(known[side:], heard[side:])], 0
    )


def total(values):
    while len(values) > 1:
        values = [x + y for x, y in zip(values[::2], values[1::2])]
    return values[0]


def hear(known, side):
    plan = meetings(side)
    used, pairs = {}, []
    for (row, z), pair in plan.items():
        for core, chip in enumerate(pair):
            from_core = used.get(chip, 1)
            used[chip] = from_core - 1
            pairs.append(((chip[0] * side + chip[1]) * 2 + from_core, (row * side + z) * 2 + core))
    return [
        lax.ppermute(known, BOTH, [(teller, hearer ^ 1) for teller, hearer in pairs]),
        lax.ppermute(known, BOTH, pairs),
    ]


def gram_body(side, view_a, view_b):
    n_col = 2 * side
    share, width = view_a.shape
    pair, half = view_b.shape
    count = share * n_col
    row = lax.axis_index("row")
    col = lax.axis_index("col")
    z = lax.shift_right_logical(col, 1)
    is_a = (col & 1) == 0
    diagonal = row == z

    got_a, got_b = sibling(view_a, n_col), sibling(view_b, n_col)
    own = jnp.where(
        is_a, jnp.concatenate([view_a, got_a], 0), jnp.concatenate([got_b, view_b], 1)
    )

    pieces, late = {}, own
    for step in range(1, side):
        pieces[step] = flip(late, side, step)
        late = jnp.where(row < (step + 1) * side, late, 0)
    pieces = [own] + [pieces[step] for step in range(1, side)]
    mine = jnp.concatenate(in_order(pieces, jnp.where(is_a, z, row)), 0)
    other = sibling(mine, n_col)

    normed, scaled = standardize(mine)
    gram = lax.dot_general(
        normed, normed, (((1,), (1,)), ((), ())), preferred_element_type=jnp.float32
    )
    normed, gram, other = lax.optimization_barrier((normed, gram, other))
    other_normed, other_scaled = standardize(other)

    normed_f = normed.astype(jnp.float32)
    other_f = other_normed.astype(jnp.float32)
    corr = jnp.mean(normed_f * other_f, 0)
    slope = jnp.where(diagonal, rounded(2.0 * (corr - 1.0)) - 2.0 * off_weight * corr, 0.0)
    extra = (slope * (normed_f - jnp.mean(normed_f, 0) - other_f * corr)).astype(jnp.bfloat16)
    part = jnp.square(1.0 - corr) - off_weight * jnp.square(corr)
    part = jnp.sum(jnp.where(diagonal, part, 0.0).reshape(-1, 128), 0, keepdims=True)

    lanes, few = width // side, 32
    i, j = (lax.broadcasted_iota(jnp.int32, (count, count), d) for d in range(2))

    def with_loss(low, part):
        part = sum(part[:, k : k + few] for k in range(0, 128, few))
        for line, half in enumerate(split(part)):
            half = jnp.pad(half, ((0, 0), (0, count - few)))
            low = jnp.where((i == count - 1 - line) & (j < few), half, low)
        return low

    def payload(images, gram, part):
        images = [images[:, i * lanes : (i + 1) * lanes] for i in range(side)]
        high, low = split(gram)
        return jnp.concatenate([jnp.concatenate(images, 0), high, with_loss(low, part)], 1)

    def images_of(step, extra):
        return lax.dynamic_slice_in_dim(extra, (row ^ step) * pair, pair, 0)

    landed = {}
    for step in (2, 1, *range(3, side)):
        ready = payload(images_of(step, extra), gram, part)
        ready, extra = lax.optimization_barrier((ready, extra))
        landed[step] = across(ready, side, step)
    landed[0] = payload(images_of(0, extra), gram, part)
    summed = total([landed[step].astype(jnp.float32) for step in range(side)])
    high, low = summed[:, lanes : lanes + count], summed[:, lanes + count :]
    part = low[count - 1 :, :few] + low[count - 2 : count - 1, :few]
    part = jnp.pad(part, ((0, 0), (0, 128 - few)))
    gram = high + low
    gram = jnp.where((i >= count - 2) & (j < few), gram.T, gram)

    sent = jnp.concatenate([summed[:, :lanes].astype(jnp.bfloat16), *split(gram)], 1)
    came = sibling(sent, n_col)
    for_a = jnp.where(is_a, came, sent)
    for_b = jnp.where(is_a, sent, came)

    slots = lax.broadcasted_iota(jnp.int32, (2 * side, 128), 0)
    known = jnp.where(slots < side, part, 1.0)
    known = jnp.where((slots & (side - 1)) == jnp.where(is_a, z, row), known, 0.0)
    known = joined(known, sibling(known, n_col))
    heard = hear(known, side)

    twice = [jnp.where(is_a, normed, other_normed)] * 2
    all_a = jnp.concatenate(twice, 0)
    twice = [jnp.where(is_a, other_normed[:, :half], normed[:, half:])] * 2
    all_b = jnp.concatenate(twice, 0)
    scaled_a = jnp.where(is_a, scaled, other_scaled)
    scaled_b = jnp.where(is_a, other_scaled[:half], scaled[half:])

    def images_in(sums):
        return jnp.concatenate([sums[i * pair : (i + 1) * pair, :lanes] for i in range(side)], 1)

    extra_a = images_in(for_a)
    extra_a = jnp.where(is_a, extra_a[:share], extra_a[share:])
    extra_b = images_in(for_b)
    extra_b = jnp.where(is_a, extra_b[:, :half], extra_b[:, half:])

    def terms(sums, twice):
        halves = sums[:, lanes : lanes + 2 * count]
        term = jnp.dot(halves, twice, preferred_element_type=jnp.float32)
        term = term * (2.0 * off_weight / count)
        return (term, jnp.mean(term, 0), jnp.mean(term * twice[:count].astype(jnp.float32), 0))

    def gradient(terms, twice, scaled, extra, start, images):
        term, first, second = terms
        term = lax.dynamic_slice_in_dim(term, start, images, 0)
        normed = lax.dynamic_slice_in_dim(twice, start, images, 0).astype(jnp.float32)
        return (scaled * (term - first - normed * second + extra.astype(jnp.float32))).astype(
            jnp.bfloat16
        )

    def whole(sums):
        sums = sums.astype(jnp.float32)
        return sums[:, lanes : lanes + count] + sums[:, lanes + count : lanes + 2 * count]

    everywhere = whole(for_a) * whole(for_b) * (off_weight / (count * count * width * side))
    everywhere = jnp.pad(jnp.sum(everywhere, 0), (0, 128 - count))
    grad_a = gradient(terms(for_a, all_a), all_a, scaled_a, extra_a, col * share, share)
    grad_b = gradient(terms(for_b, all_b), all_b, scaled_b, extra_b, row * pair, pair)

    heard, grad_a, grad_b, everywhere = lax.optimization_barrier((heard, grad_a, grad_b, everywhere))
    known = joined(joined(known, heard[0]), heard[1])
    loss = jnp.sum(everywhere + jnp.sum(known[:side], 0) * (1.0 / (width * side)))
    return (loss, grad_a, grad_b)


def solution(mesh):
    in_specs = (P("col", "row"), P("row", "col"))
    out_specs = (P(), P("col", "row"), P("row", "col"))
    n_row, n_col = mesh.shape["row"], mesh.shape["col"]
    square = n_col == 2 * n_row and n_row & (n_row - 1) == 0

    def body(view_a, view_b):
        share, width = view_a.shape
        count = share * n_col
        fits = view_b.shape == (2 * share, width // 2) and width % (128 * n_row) == 0
        fits = fits and share % 8 == 0 and count <= 128 and 2 * count % 128 == 0
        if square and fits and meetings(n_row):
            return gram_body(n_row, view_a, view_b)
        return tiled_body(view_a, view_b)

    return jax.shard_map(body, mesh=mesh, in_specs=in_specs, out_specs=out_specs, check_vma=False)
```
